32 devices in a mesh: groups: 2 (over y), fsdp: 4 (over z), tp: 4 (over x, core).
Axes of the slice: x: 2, y: 2, z: 4, core: 2. Of those that a mesh axis runs over, the one named last changes fastest.
Arguments:
- activations: bfloat16 [1024, 8192], P(('groups', 'fsdp'), 'tp'), parts along dimension 0, may hold values from -6 to 6
- key_value_weight: bfloat16 [2048, 8192], P('fsdp', 'tp'), may hold values from -0.0625 to 0.0625
- token_adapter_index: int32 [1024, 1], P(('groups', 'fsdp')), parts along dimension 0, may hold values from 0 to 3; in each aligned block of 128 rows (0 to 127, 128 to 255, ...) at most 64 rows name the same one
- adapter_down_weight: bfloat16 [4, 64, 8192], P('fsdp', None, 'tp'), may hold values from -0.0625 to 0.0625
- adapter_up_weight: bfloat16 [4, 64, 2048], P('fsdp', None, 'tp'), may hold values from -0.19921875 to 0.19921875
- cotangent: bfloat16 [1024, 2048], P(('groups', 'fsdp'), 'tp'), parts along dimension 0, may hold values from -6 to 6
Outputs:
- key_value_output: bfloat16 [1024, 2048], P(('groups', 'fsdp'), 'tp'), parts along dimension 0
- input_gradient: bfloat16 [1024, 8192], P(('groups', 'fsdp'), 'tp'), parts along dimension 0
- grad_down: float32 [8, 64, 8192], P(('groups', 'fsdp'), None, 'tp'), parts along dimension 0
- up_gradient: float32 [8, 64, 2048], P(('groups', 'fsdp'), None, 'tp'), parts along dimension 0
The draws below stay inside these ranges and needn't reach their ends.
There are 2 independent parts, one for each index of `groups`. The reference program is written for one: setup_inputs(seed, part) draws one part's arguments, and reference() takes and returns one part's arrays. A program takes and returns all parts, laid end to end along the dimension named above; an argument that names none is the same for every part. Nothing has to cross between parts.
Inputs may be any that keep to these rules, and one draw needn't show every extreme that they name: `token_adapter_index`: among the 128 tokens of one index of fsdp no adapter appears more than 64 times.
All inputs are finite; a program needn't handle non-finite values.
Results may differ from the reference program's by a relative error of at most 0.013.
Values may be sent and summed in bfloat16 or wider, within the bound.
No kernel may reach another device: no remote copies, remote signals or barrier semaphores. Data moves between devices by JAX's collectives and lax.ppermute only.
A program may use at most 64 MiB of HBM per device.

```python
import math
import jax
import jax.numpy as jnp
import numpy as np
from jax import lax

MODEL_WIDTH = 8192
KEY_VALUE_WIDTH = 2048
ADAPTER_RANK = 64
TOK_DEV = 128
TOKENS = 512
ADAPTER_COUNT = 4
CAP = 64
N_TP = 4


def level_of(rng, dims, split, least, high):
    def one(dim, shards_of):
        heights = jax.random.uniform(jax.random.fold_in(jax.random.fold_in(rng, 6), dim), (shards_of,), jnp.float32, least / len(split), high / len(split))
        return jnp.repeat(jnp.exp(heights), dims[dim] // shards_of).reshape((-1,) + (1,) * (len(dims) - dim - 1))

    gain = one(*split[0])
    for cut in split[1:]:
        gain = gain * one(*cut)
    return gain


def assign_block(stream_key, own, number, rows, amount, top, limit, lean):
    ranking = jax.random.permutation(stream_key, amount)
    packed, common = shares(amount, rows * top, limit, lean, True), shares(amount, rows * top, limit, lean, False)
    places = jnp.arange(amount)

    def named(tallies, rotation):
        used = int((tallies > 0).sum())
        fixed = max(1, used // 4)
        moved = fixed + (places - fixed + rotation * (used - fixed)) % max(1, amount - fixed)
        return jnp.zeros((amount,), jnp.int32).at[ranking[jnp.where(places < fixed, places, moved)]].set(jnp.asarray(tallies, jnp.int32))

    tallies = jnp.where(number % 4 == 0, named(packed, number // 4), named(common, number - number // 4 - 1))
    mixed = jax.random.permutation(jax.random.fold_in(own, 3), amount)
    source_of, receiver = mixed[0:amount // 2 * 2:2], mixed[1:amount // 2 * 2:2]
    room = jnp.minimum(tallies[source_of] - 1, limit - tallies[receiver]) // 2
    room = jnp.where((source_of == ranking[0]) | (receiver == ranking[0]) | (tallies[receiver] == 0), 0, jnp.maximum(room, 0))
    moved = jax.random.randint(jax.random.fold_in(own, 4), (amount // 2,), 0, 1 << 20) % (room + 1)
    tallies = tallies.at[source_of].add(-moved).at[receiver].add(moved)
    members = jnp.searchsorted(jnp.cumsum(tallies), jnp.arange(rows * top), side="right").astype(jnp.int32)
    table = members.reshape(top, rows).T
    table = table[jax.random.permutation(jax.random.fold_in(own, 1), rows)]
    rotation = jax.random.randint(jax.random.fold_in(own, 2), (rows, 1), 0, top)
    return jnp.take_along_axis(table, (jnp.arange(top)[None, :] + rotation) % top, axis=1)


def shares(number_of, total, reach, slope, full):
    weights = [(1 << 20) // math.isqrt(grade ** slope) + 1 for grade in range(1, number_of + 1)]
    largest = reach if full else min(reach, max(-(-total // number_of), total * weights[0] // sum(weights)))
    least = 1 if total - largest >= number_of - 1 else 0
    holding, spare = [largest] + [least] * (number_of - 1), total - largest - least * (number_of - 1)
    while spare > 0:
        movable = [i for i in range(1, number_of) if holding[i] < largest] or [i for i in range(1, number_of) if holding[i] < reach]
        whole, remaining = sum([weights[i] for i in movable]), spare
        for i in movable:
            addition = min(reach - holding[i], max(1, remaining * weights[i] // whole), spare)
            holding[i] = holding[i] + addition
            spare = spare - addition
    return np.array(holding)


def centred(own_key, extent, scale, reach, pieces=(), kind=jnp.bfloat16):
    result = scale * jax.random.normal(own_key, extent, jnp.float32)
    if pieces:
        result = result * level_of(own_key, extent, pieces, -0.22, 0.18)
    return jnp.clip(result, -reach, reach).astype(kind)


def setup_inputs(seed: int = 0, part: int = 0) -> dict:
    streams_of = jax.random.split(jax.random.key(seed), 7)
    own_keys = jax.random.split(jax.random.fold_in(streams_of[6], part), 7)
    activations = centred(own_keys[0], (TOKENS, MODEL_WIDTH), 1.0, 6.0, ((0, 4), (1, 4)))
    key_value_weight = centred(streams_of[1], (KEY_VALUE_WIDTH, MODEL_WIDTH), MODEL_WIDTH ** -0.5, 0.0625, ((0, 4), (1, 4)))
    token_adapter_index_keys = jax.random.split(jax.random.fold_in(own_keys[2], 1), TOKENS // TOK_DEV)
    token_adapter_index_turns = jax.random.permutation(jax.random.fold_in(own_keys[2], 3), TOKENS // TOK_DEV)
    token_adapter_index = jax.vmap(lambda own, number: assign_block(jax.random.fold_in(own_keys[2], 2), own, number, TOK_DEV, ADAPTER_COUNT, 1, CAP, 2))(token_adapter_index_keys, token_adapter_index_turns).reshape((TOKENS, 1))
    adapter_down_weight = centred(streams_of[3], (ADAPTER_COUNT, ADAPTER_RANK, MODEL_WIDTH), MODEL_WIDTH ** -0.5, 0.0625, ((0, 4), (2, 4)))
    adapter_up_weight = centred(streams_of[4], (ADAPTER_COUNT, ADAPTER_RANK, KEY_VALUE_WIDTH), 0.03, 0.19921875, ((0, 4), (2, 4)))
    cotangent = centred(own_keys[5], (TOKENS, KEY_VALUE_WIDTH), 1.0, 6.0, ((0, 4), (1, 4)))
    return {"activations": activations, "key_value_weight": key_value_weight, "token_adapter_index": token_adapter_index, "adapter_down_weight": adapter_down_weight, "adapter_up_weight": adapter_up_weight, "cotangent": cotangent}


adapter_scale = 2.0


def broaden_rows(values):
    return lax.optimization_barrier(values).astype(jnp.float32)


def reference(activations, key_value_weight, token_adapter_index, adapter_down_weight, adapter_up_weight, cotangent):
    width = MODEL_WIDTH // N_TP
    base_output = jnp.zeros((TOKENS, KEY_VALUE_WIDTH), jnp.float32)
    for block in range(N_TP):
        part = jnp.dot(activations[:, block * width:(block + 1) * width], key_value_weight[:, block * width:(block + 1) * width].T, preferred_element_type=jnp.float32)
        base_output = base_output + broaden_rows(part.astype(jnp.bfloat16))
    shard_member = (token_adapter_index[:, 0][:, None] == jnp.arange(ADAPTER_COUNT, dtype=jnp.int32)[None, :]).astype(jnp.float32)
    down_joined = adapter_down_weight.reshape(ADAPTER_COUNT * ADAPTER_RANK, MODEL_WIDTH)
    up_joined = adapter_up_weight.reshape(ADAPTER_COUNT * ADAPTER_RANK, KEY_VALUE_WIDTH)
    low_all = jnp.dot(activations, down_joined.T, preferred_element_type=jnp.float32).reshape(TOKENS, ADAPTER_COUNT, ADAPTER_RANK)
    rank_activation = jnp.einsum("dpi,dp->di", low_all, shard_member).astype(jnp.bfloat16)
    scatter_rows = (shard_member[:, :, None] * rank_activation.astype(jnp.float32)[:, None, :]).reshape(TOKENS, ADAPTER_COUNT * ADAPTER_RANK).astype(jnp.bfloat16)
    adapter_output = (adapter_scale * jnp.dot(scatter_rows, up_joined, preferred_element_type=jnp.float32)).astype(jnp.bfloat16)
    key_value_output = (base_output + broaden_rows(adapter_output)).astype(jnp.bfloat16)
    backward_gathered = jnp.dot(cotangent, up_joined.T, preferred_element_type=jnp.float32).reshape(TOKENS, ADAPTER_COUNT, ADAPTER_RANK)
    backward_result = (adapter_scale * jnp.einsum("dpi,dp->di", backward_gathered, shard_member)).astype(jnp.bfloat16)
    backward_scatter = (shard_member[:, :, None] * backward_result.astype(jnp.float32)[:, None, :]).reshape(TOKENS, ADAPTER_COUNT * ADAPTER_RANK).astype(jnp.bfloat16)
    adapter_input = jnp.dot(backward_scatter, down_joined, preferred_element_type=jnp.float32).astype(jnp.bfloat16)
    base_gradient = jnp.dot(cotangent, key_value_weight, preferred_element_type=jnp.float32)
    input_gradient = (base_gradient + broaden_rows(adapter_input)).astype(jnp.bfloat16)
    grad_down = jnp.dot(backward_scatter.T, activations, preferred_element_type=jnp.float32).reshape(ADAPTER_COUNT, ADAPTER_RANK, MODEL_WIDTH)
    up_gradient = (adapter_scale * jnp.dot(scatter_rows.T, cotangent, preferred_element_type=jnp.float32)).reshape(ADAPTER_COUNT, ADAPTER_RANK, KEY_VALUE_WIDTH)
    return key_value_output, input_gradient, grad_down, up_gradient
```

```python
import jax
import jax.numpy as jnp
from jax import lax
from jax.sharding import PartitionSpec as P

adapter_scale = 2.0
f32 = jnp.float32
bf16 = jnp.bfloat16


def placement_matrix(token_adapter_index, adapter_holders, slot_capacity):
    owner_of = token_adapter_index[:, 0]
    shard_member = (
        owner_of[:, None] == jnp.arange(adapter_holders, dtype=jnp.int32)[None, :]
    ).astype(jnp.int32)
    earlier = jnp.cumsum(shard_member, axis=0) - shard_member
    within = jnp.sum(earlier * shard_member, axis=1)
    target = owner_of * slot_capacity + within
    return (
        jnp.arange(adapter_holders * slot_capacity, dtype=jnp.int32)[:, None] == target[None, :]
    ).astype(jnp.bfloat16)


def pack_rows(placing, values, adapter_holders):
    packed = jnp.dot(placing, values, preferred_element_type=jnp.float32).astype(jnp.bfloat16)
    return packed.reshape(adapter_holders, -1, values.shape[1])


def unpack_rows(placing, returned):
    flat = returned.reshape(-1, returned.shape[2])
    return jnp.einsum("st,sk->tk", placing, flat, preferred_element_type=jnp.float32)


def gathered_plan(
    activations,
    key_value_weight,
    token_adapter_index,
    adapter_down_weight,
    adapter_up_weight,
    cotangent,
):
    adapter_holders = lax.axis_size("fsdp")
    tok_rows = activations.shape[0]
    slot_capacity = 2 * tok_rows // adapter_holders
    feature_width = activations.shape[1]
    output_width = cotangent.shape[1]
    placing = placement_matrix(token_adapter_index, adapter_holders, slot_capacity)
    down_resident = adapter_down_weight[0]
    up_resident = adapter_up_weight[0]
    whole_cot = lax.all_gather(cotangent, "tp", axis=1, tiled=True)
    whole_weight = lax.all_gather(key_value_weight, "fsdp", axis=0, tiled=True)
    partial_value = jnp.dot(activations, whole_weight.T, preferred_element_type=jnp.float32)
    base_gradient = jnp.dot(whole_cot, whole_weight, preferred_element_type=jnp.float32)
    base_output = lax.psum_scatter(
        partial_value.astype(jnp.bfloat16), "tp", scatter_dimension=1, tiled=True
    ).astype(jnp.float32)
    rows_send = pack_rows(placing, activations, adapter_holders)
    cot_send = pack_rows(placing, cotangent, adapter_holders)
    rows_recv = lax.all_to_all(rows_send, "fsdp", split_axis=0, concat_axis=0, tiled=True)
    rows_flat = rows_recv.reshape(-1, feature_width)
    low_part = jnp.dot(rows_flat, down_resident.T, preferred_element_type=jnp.float32)
    rank_activation = lax.psum(low_part.astype(jnp.bfloat16), "tp")
    adapter_output = (
        adapter_scale * jnp.dot(rank_activation, up_resident, preferred_element_type=jnp.float32)
    ).astype(jnp.bfloat16)
    out_back = lax.all_to_all(
        adapter_output.reshape(adapter_holders, slot_capacity, output_width),
        "fsdp",
        split_axis=0,
        concat_axis=0,
        tiled=True,
    )
    cot_recv = lax.all_to_all(cot_send, "fsdp", split_axis=0, concat_axis=0, tiled=True)
    flat_output_gradient = cot_recv.reshape(-1, output_width)
    backward_piece = adapter_scale * jnp.dot(
        flat_output_gradient, up_resident.T, preferred_element_type=jnp.float32
    )
    backward_result = lax.psum(backward_piece.astype(jnp.bfloat16), "tp")
    adapter_input = jnp.dot(
        backward_result, down_resident, preferred_element_type=jnp.float32
    ).astype(jnp.bfloat16)
    in_back = lax.all_to_all(
        adapter_input.reshape(adapter_holders, slot_capacity, feature_width),
        "fsdp",
        split_axis=0,
        concat_axis=0,
        tiled=True,
    )
    grad_down = jnp.einsum(
        "sr,sd->rd", backward_result, rows_flat, preferred_element_type=jnp.float32
    )
    up_gradient = adapter_scale * jnp.einsum(
        "sr,sk->rk", rank_activation, flat_output_gradient, preferred_element_type=jnp.float32
    )
    key_value_output = (base_output + unpack_rows(placing, out_back)).astype(jnp.bfloat16)
    input_gradient = (base_gradient + unpack_rows(placing, in_back)).astype(jnp.bfloat16)
    return (key_value_output, input_gradient, grad_down[None], up_gradient[None])


def nn(a, b):
    return lax.dot_general(a, b, (((1,), (0,)), ((), ())), preferred_element_type=f32)


def nt(a, b):
    return lax.dot_general(a, b, (((1,), (1,)), ((), ())), preferred_element_type=f32)


def tn(a, b):
    return lax.dot_general(a, b, (((0,), (0,)), ((), ())), preferred_element_type=f32)


def swap(x, axis, bit):
    return lax.ppermute(x, axis, [(i, i ^ bit) for i in range(lax.axis_size(axis))])


def both(x, pairs):
    flat = [(4 * a[0] + 2 * a[1] + a[2], 4 * b[0] + 2 * b[1] + b[2]) for a, b in pairs]
    return lax.ppermute(x, ("fsdp", "tp"), flat)


def tp_sum(part):
    rows = part.shape[0] // 2
    wide = jnp.concatenate([part[:rows], part[rows:]], axis=1)
    parts = lax.all_gather(wide, "tp", axis=0)
    total = jnp.sum(parts.astype(f32), axis=0)
    return jnp.concatenate([total[:, : part.shape[1]], total[:, part.shape[1] :]], axis=0)


CHUNKS = 2


def pair_plan(
    activations,
    key_value_weight,
    token_adapter_index,
    adapter_down_weight,
    adapter_up_weight,
    cotangent,
):
    z = lax.axis_index("fsdp")
    y = lax.axis_index("groups")
    t = lax.axis_index("tp")
    x, c = t // 2, t % 2
    pair = z // 2
    in_pair = x == pair
    on_own = c == z % 2
    rows, width = key_value_weight.shape
    toks = activations.shape[0]
    half = rows // 2
    down = adapter_down_weight[0]
    up = adapter_up_weight[0]
    rank = down.shape[0]
    places = [(zz, xx, cc) for zz in range(4) for xx in range(2) for cc in range(2)]

    cot2 = jnp.concatenate([cotangent, swap(cotangent, "fsdp", 2)], axis=0)
    index2 = jnp.concatenate([token_adapter_index, swap(token_adapter_index, "fsdp", 2)], axis=0)
    up_sib = swap(up, "fsdp", 1)

    step = width // CHUNKS
    w_mine = lax.dynamic_slice(key_value_weight, (y * half, 0), (half, width))
    d_mine = lax.dynamic_slice(down, (y * (rank // 2), 0), (rank // 2, width))
    near, far = [], []
    for k in range(CHUNKS):
        piece = w_mine[:, k * step : (k + 1) * step]
        if k == 0:
            piece = jnp.concatenate(
                [d_mine[:, j * step : (j + 1) * step] for j in range(CHUNKS)] + [piece], axis=0
            )
        got = swap(piece, "fsdp", 1)
        near.append(got)
        far.append(swap(got, "groups", 1))
        if k == 0:
            act2 = jnp.concatenate([activations, swap(activations, "fsdp", 2)], axis=0)
    cut = rank // 2 * CHUNKS

    def down_of(piece):
        return jnp.concatenate(
            [piece[j * (rank // 2) : (j + 1) * (rank // 2)] for j in range(CHUNKS)], axis=1
        )

    d_near, d_far = down_of(near[0]), down_of(far[0])
    near[0], far[0] = near[0][cut:], far[0][cut:]

    own = index2 == z
    sib = index2 == (z ^ 1)
    back_part = adapter_scale * jnp.where(
        own, nt(cot2, up), jnp.where(sib, nt(cot2, up_sib), 0.0)
    )
    back = tp_sum(back_part.astype(bf16)).astype(bf16)
    back_own = jnp.where(own, back, 0).astype(bf16)
    back_sib = jnp.where(sib, back, 0).astype(bf16)

    sent = both(
        cot2, [((a, b, d), (a, 1 - b, d)) for a, b, d in places if b == a // 2]
    )
    block = jnp.where(in_pair, cot2, sent)
    other = swap(block, "tp", 1)
    c_own = jnp.where(on_own, block, other)
    c_sib = jnp.where(on_own, other, block)
    c_near = lax.dynamic_slice(c_sib, (0, y * half), (2 * toks, half))
    c_far = lax.dynamic_slice(c_sib, (0, (1 - y) * half), (2 * toks, half))
    hr = rank // 2
    b_near = lax.dynamic_slice(back_sib, (0, y * hr), (2 * toks, hr))
    b_far = lax.dynamic_slice(back_sib, (0, (1 - y) * hr), (2 * toks, hr))

    grads = []
    for k in range(CHUNKS):
        cols = slice(k * step, (k + 1) * step)
        g = (
            nn(c_own, key_value_weight[:, cols])
            + nn(c_near, near[k])
            + nn(c_far, far[k])
            + nn(back_own, down[:, cols])
            + nn(b_near, d_near[:, cols])
            + nn(b_far, d_far[:, cols])
        )
        grads.append((g[:toks] + swap(g[toks:].astype(bf16), "fsdp", 2)).astype(bf16))
    input_gradient = jnp.concatenate(grads, axis=1)

    low_far, low_near = nt(act2, d_far), nt(act2, d_near)
    first = y == 0
    low_sib = jnp.concatenate(
        [jnp.where(first, low_near, low_far), jnp.where(first, low_far, low_near)], axis=1
    )
    low_part = jnp.where(own, nt(act2, down), jnp.where(sib, low_sib, 0.0))
    low = tp_sum(low_part.astype(bf16)).astype(bf16)
    low_own = jnp.where(own, low, 0).astype(bf16)
    low_other = jnp.where(sib, low, 0).astype(bf16)
    lora = (adapter_scale * (nn(low_own, up) + nn(low_other, up_sib))).astype(bf16)
    lora_got = swap(lora[toks:], "fsdp", 2)

    gd_sib = tn(back_sib, act2).astype(bf16)
    gu_sib = (adapter_scale * tn(low_other, cot2)).astype(bf16)
    got = swap(jnp.concatenate([gd_sib, gu_sib], axis=1), "fsdp", 1)
    grad_down = tn(back_own, act2) + got[:, :width]
    up_gradient = adapter_scale * tn(low_own, cot2) + got[:, width:]

    p_own = nt(act2, key_value_weight)
    p_near = p_far = 0.0
    for k in range(CHUNKS):
        cols = slice(k * step, (k + 1) * step)
        p_near = p_near + nt(act2[:, cols], near[k])
        p_far = p_far + nt(act2[:, cols], far[k])
    p_sib = jnp.concatenate(
        [jnp.where(first, p_near, p_far), jnp.where(first, p_far, p_near)], axis=1
    )
    keep = jnp.where(on_own, p_own, p_sib)
    give = jnp.where(on_own, p_sib, p_own).astype(bf16)
    held = (keep + swap(give, "tp", 1)).astype(bf16)
    here, there = held[:toks], held[toks:]
    one = both(
        jnp.where(in_pair, there, here),
        [((a, b, d), (a ^ 2, b, d) if b == a // 2 else (a, 1 - b, d)) for a, b, d in places],
    )
    two = both(there, [((a, b, d), (a ^ 2, 1 - b, d)) for a, b, d in places if b != a // 2])
    base = one.astype(f32) + jnp.where(in_pair, here, two).astype(f32)
    key_value_output = (base + lora[:toks].astype(f32) + lora_got.astype(f32)).astype(bf16)
    return (key_value_output, input_gradient, grad_down[None], up_gradient[None])


def solution(mesh):
    paired = mesh.shape["fsdp"] == 4 and mesh.shape["tp"] == 4 and mesh.shape["groups"] == 2
    return jax.shard_map(
        pair_plan if paired else gathered_plan,
        mesh=mesh,
        in_specs=(
            P(("groups", "fsdp"), "tp"),
            P("fsdp", "tp"),
            P(("groups", "fsdp"), None),
            P("fsdp", None, "tp"),
            P("fsdp", None, "tp"),
            P(("groups", "fsdp"), "tp"),
        ),
        out_specs=(
            P(("groups", "fsdp"), "tp"),
            P(("groups", "fsdp"), "tp"),
            P(("groups", "fsdp"), None, "tp"),
            P(("groups", "fsdp"), None, "tp"),
        ),
        check_vma=False,
    )
```

```python
import jax
import jax.numpy as jnp
from jax import lax
from jax.experimental import pallas as pl
from jax.experimental.pallas import tpu as pltpu
from jax.sharding import PartitionSpec as P

adapter_scale = 2.0
f32 = jnp.float32
bf16 = jnp.bfloat16


def placement_matrix(token_adapter_index, adapter_holders, slot_capacity):
    owner_of = token_adapter_index[:, 0]
    shard_member = (
        owner_of[:, None] == jnp.arange(adapter_holders, dtype=jnp.int32)[None, :]
    ).astype(jnp.int32)
    earlier = jnp.cumsum(shard_member, axis=0) - shard_member
    within = jnp.sum(earlier * shard_member, axis=1)
    target = owner_of * slot_capacity + within
    return (
        jnp.arange(adapter_holders * slot_capacity, dtype=jnp.int32)[:, None] == target[None, :]
    ).astype(jnp.bfloat16)


def pack_rows(placing, values, adapter_holders):
    packed = jnp.dot(placing, values, preferred_element_type=jnp.float32).astype(jnp.bfloat16)
    return packed.reshape(adapter_holders, -1, values.shape[1])


def unpack_rows(placing, returned):
    flat = returned.reshape(-1, returned.shape[2])
    return jnp.einsum("st,sk->tk", placing, flat, preferred_element_type=jnp.float32)


def gathered_plan(
    activations,
    key_value_weight,
    token_adapter_index,
    adapter_down_weight,
    adapter_up_weight,
    cotangent,
):
    adapter_holders = lax.axis_size("fsdp")
    tok_rows = activations.shape[0]
    slot_capacity = 2 * tok_rows // adapter_holders
    feature_width = activations.shape[1]
    output_width = cotangent.shape[1]
    placing = placement_matrix(token_adapter_index, adapter_holders, slot_capacity)
    down_resident = adapter_down_weight[0]
    up_resident = adapter_up_weight[0]
    whole_cot = lax.all_gather(cotangent, "tp", axis=1, tiled=True)
    whole_weight = lax.all_gather(key_value_weight, "fsdp", axis=0, tiled=True)
    partial_value = jnp.dot(activations, whole_weight.T, preferred_element_type=jnp.float32)
    base_gradient = jnp.dot(whole_cot, whole_weight, preferred_element_type=jnp.float32)
    base_output = lax.psum_scatter(
        partial_value.astype(jnp.bfloat16), "tp", scatter_dimension=1, tiled=True
    ).astype(jnp.float32)
    rows_send = pack_rows(placing, activations, adapter_holders)
    cot_send = pack_rows(placing, cotangent, adapter_holders)
    rows_recv = lax.all_to_all(rows_send, "fsdp", split_axis=0, concat_axis=0, tiled=True)
    rows_flat = rows_recv.reshape(-1, feature_width)
    low_part = jnp.dot(rows_flat, down_resident.T, preferred_element_type=jnp.float32)
    rank_activation = lax.psum(low_part.astype(jnp.bfloat16), "tp")
    adapter_output = (
        adapter_scale * jnp.dot(rank_activation, up_resident, preferred_element_type=jnp.float32)
    ).astype(jnp.bfloat16)
    out_back = lax.all_to_all(
        adapter_output.reshape(adapter_holders, slot_capacity, output_width),
        "fsdp",
        split_axis=0,
        concat_axis=0,
        tiled=True,
    )
    cot_recv = lax.all_to_all(cot_send, "fsdp", split_axis=0, concat_axis=0, tiled=True)
    flat_output_gradient = cot_recv.reshape(-1, output_width)
    backward_piece = adapter_scale * jnp.dot(
        flat_output_gradient, up_resident.T, preferred_element_type=jnp.float32
    )
    backward_result = lax.psum(backward_piece.astype(jnp.bfloat16), "tp")
    adapter_input = jnp.dot(
        backward_result, down_resident, preferred_element_type=jnp.float32
    ).astype(jnp.bfloat16)
    in_back = lax.all_to_all(
        adapter_input.reshape(adapter_holders, slot_capacity, feature_width),
        "fsdp",
        split_axis=0,
        concat_axis=0,
        tiled=True,
    )
    grad_down = jnp.einsum(
        "sr,sd->rd", backward_result, rows_flat, preferred_element_type=jnp.float32
    )
    up_gradient = adapter_scale * jnp.einsum(
        "sr,sk->rk", rank_activation, flat_output_gradient, preferred_element_type=jnp.float32
    )
    key_value_output = (base_output + unpack_rows(placing, out_back)).astype(jnp.bfloat16)
    input_gradient = (base_gradient + unpack_rows(placing, in_back)).astype(jnp.bfloat16)
    return (key_value_output, input_gradient, grad_down[None], up_gradient[None])


def nn(a, b):
    return lax.dot_general(a, b, (((1,), (0,)), ((), ())), preferred_element_type=f32)


def nt(a, b):
    return lax.dot_general(a, b, (((1,), (1,)), ((), ())), preferred_element_type=f32)


def tn(a, b):
    return lax.dot_general(a, b, (((0,), (0,)), ((), ())), preferred_element_type=f32)


def rows2(a, b):
    return jnp.concatenate([a, b], axis=0)


def swap(x, axis, bit):
    return lax.ppermute(x, axis, [(i, i ^ bit) for i in range(lax.axis_size(axis))])


def both(x, pairs):
    flat = [(4 * a[0] + 2 * a[1] + a[2], 4 * b[0] + 2 * b[1] + b[2]) for a, b in pairs]
    return lax.ppermute(x, ("fsdp", "tp"), flat)


Y, Z, IN_PAIR, ON_OWN = range(4)


def local_kernel(body, outs, where, *args):
    single = not isinstance(outs, list)
    shapes = [jax.ShapeDtypeStruct(s, d) for s, d in ([outs] if single else outs)]
    got = pl.pallas_call(
        body,
        out_shape=shapes,
        in_specs=[pl.BlockSpec(memory_space=pltpu.SMEM)]
        + [pl.BlockSpec(memory_space=pltpu.VMEM)] * len(args),
        out_specs=[pl.BlockSpec(memory_space=pltpu.VMEM)] * len(shapes),
        compiler_params=pltpu.CompilerParams(vmem_limit_bytes=24 * 1024 * 1024),
        cost_estimate=pl.CostEstimate(flops=1000, bytes_accessed=1000, transcendentals=0),
    )(where, *args)
    return got[0] if single else got


def member(where, idx, rank):
    lane = lax.broadcasted_iota(jnp.int32, (idx.shape[0], 2 * rank), 1)
    z = where[Z]
    return idx == jnp.where(lane < rank, z, z ^ 1)


def back_kernel(where, cot, cot_got, idx, idx_got, up, up_sib, out):
    width = cot.shape[1]
    cot2 = rows2(cot[...], cot_got[...])
    part = adapter_scale * nt(cot2, rows2(up[...], up_sib[...]))
    mine = member(where, rows2(idx[...], idx_got[...]), up.shape[0])
    out[:, :width] = cot2
    out[:, width:] = jnp.where(mine, part, 0.0).astype(bf16)


def block_kernel(where, mine, got, out):
    width = out.shape[1] - 128
    in_pair = jnp.full((1, 1), where[IN_PAIR], jnp.int32) == 1
    out[:, :width] = jnp.where(in_pair, mine[:, :width], got[:, :width])
    out[:, width:] = (mine[:, width:].astype(f32) + got[:, width:].astype(f32)).astype(bf16)


def pair_blocks(where, mine, got):
    width = mine.shape[1] - 128
    on_own = jnp.full((1, 1), where[ON_OWN], jnp.int32) == 1
    a, b = mine[:, :width], got[:, :width]
    return jnp.where(on_own, a, b), jnp.where(on_own, b, a)


def whole_back(mine, got):
    width = mine.shape[1] - 128
    return (mine[:, width:].astype(f32) + got[:, width:].astype(f32)).astype(bf16)


def gradient_kernel(where, mine, got, weight, down, first, second, top, bottom):
    rank = down.shape[0]
    half = second.shape[0]
    c_own, c_sib = pair_blocks(where, mine, got)
    back = whole_back(mine, got)
    g = nn(c_own, weight[...])
    g += nn(c_sib[:, :half], first[rank:, :])
    g += nn(c_sib[:, half:], second[...])
    g += nn(back, rows2(down[...], first[:rank, :]))
    toks = top.shape[0]
    top[...] = g[:toks]
    bottom[...] = g[toks:].astype(bf16)


def gradient_half(where, side, mine, got, weight, down, first, second):
    toks, tile = mine.shape[0] // 2, 512
    steps = first.shape[1] // tile
    whole = lambda a: pl.BlockSpec(a.shape, lambda j, s: (0, 0))
    by_side = lambda a: pl.BlockSpec((a.shape[0], tile), lambda j, s: (0, s[4] * steps + j))
    tiled = lambda n: pl.BlockSpec((n, tile), lambda j, s: (0, j))
    return pl.pallas_call(
        gradient_kernel,
        grid_spec=pltpu.PrefetchScalarGridSpec(
            num_scalar_prefetch=1,
            grid=(steps,),
            in_specs=[
                whole(mine),
                whole(got),
                by_side(weight),
                by_side(down),
                tiled(first.shape[0]),
                tiled(second.shape[0]),
            ],
            out_specs=[tiled(toks), tiled(toks)],
        ),
        out_shape=[
            jax.ShapeDtypeStruct((toks, steps * tile), f32),
            jax.ShapeDtypeStruct((toks, steps * tile), bf16),
        ],
        compiler_params=pltpu.CompilerParams(vmem_limit_bytes=24 * 1024 * 1024),
        cost_estimate=pl.CostEstimate(flops=1000, bytes_accessed=1000, transcendentals=0),
    )(jnp.concatenate([where, side[None]]), mine, got, weight, down, first, second)


def gradient_end_kernel(where, near, near_got, far, far_got, out):
    half = near.shape[1]
    y = where[Y]
    at = pl.ds(pl.multiple_of(y * half, half), half)
    out[:, at] = (near[...] + near_got[...].astype(f32)).astype(bf16)
    at = pl.ds(pl.multiple_of((1 - y) * half, half), half)
    out[:, at] = (far[...] + far_got[...].astype(f32)).astype(bf16)


def low_kernel(where, act, act_got, idx, idx_got, down, near, far, out):
    rank, half = down.shape[0], near.shape[1]
    y = where[Y]
    at_near = pl.ds(pl.multiple_of(y * half, half), half)
    at_far = pl.ds(pl.multiple_of((1 - y) * half, half), half)
    part = nt(rows2(act[:, at_near], act_got[:, at_near]), rows2(down[:, at_near], near[:rank, :]))
    part += nt(rows2(act[:, at_far], act_got[:, at_far]), rows2(down[:, at_far], far[:rank, :]))
    mine = member(where, rows2(idx[...], idx_got[...]), rank)
    out[...] = jnp.where(mine, part, 0.0).astype(bf16)


def adapter_kernel(
    where, low, low_got, mine, got, act, act_got, cot, cot_got, up, up_sib,
    lora, lora_far, down_own, up_own, sib,
):
    rank, width, toks = up.shape[0], act.shape[1], act.shape[0]
    whole_low = (low[...].astype(f32) + low_got[...].astype(f32)).astype(bf16)
    out = (adapter_scale * nn(whole_low, rows2(up[...], up_sib[...]))).astype(bf16)
    lora[...] = out[:toks]
    lora_far[...] = out[toks:]
    grad = tn(whole_back(mine, got), rows2(act[...], act_got[...]))
    down_own[...] = grad[:rank]
    sib[:, :width] = grad[rank:].astype(bf16)
    grad = adapter_scale * tn(whole_low, rows2(cot[...], cot_got[...]))
    up_own[...] = grad[:rank]
    sib[:, width:] = grad[rank:].astype(bf16)


def adapter_end_kernel(where, down_own, up_own, got, down_out, up_out):
    width = down_own.shape[1]
    down_out[0] = down_own[...] + got[:, :width].astype(f32)
    up_out[0] = up_own[...] + got[:, width:].astype(f32)


def base_near_kernel(where, act, act_got, weight, first, second, out):
    rows, half = weight.shape[0], second.shape[0]
    cut = first.shape[0] - half
    wide = first.shape[1]
    at = pl.ds(pl.multiple_of(where[Y] * wide, wide), wide)
    near = rows2(act[:, at], act_got[:, at])
    out[:, :rows] = nt(rows2(act[...], act_got[...]), weight[...])
    out[:, rows : rows + half] = nt(near, first[cut:, :])
    out[:, rows + half :] = nt(near, second[...])


def base_far_kernel(where, part, act, act_got, first, second, keep, give):
    half = second.shape[0]
    rows = 2 * half
    cut = first.shape[0] - half
    wide = first.shape[1]
    at = pl.ds(pl.multiple_of((1 - where[Y]) * wide, wide), wide)
    far = rows2(act[:, at], act_got[:, at])
    on_own = jnp.full((1, 1), where[ON_OWN], jnp.int32) == 1
    for k, block in ((0, first[cut:, :]), (1, second[...])):
        at = slice(k * half, (k + 1) * half)
        mine = part[:, k * half : (k + 1) * half]
        other = part[:, rows + k * half : rows + (k + 1) * half] + nt(far, block)
        keep[:, at] = jnp.where(on_own, mine, other)
        give[:, at] = jnp.where(on_own, other, mine).astype(bf16)


def held_kernel(where, keep, got, here, there, turn):
    toks = here.shape[0]
    held = (keep[...] + got[...].astype(f32)).astype(bf16)
    in_pair = jnp.full((1, 1), where[IN_PAIR], jnp.int32) == 1
    here[...] = held[:toks]
    there[...] = held[toks:]
    turn[...] = jnp.where(in_pair, held[toks:], held[:toks])


def output_kernel(where, one, two, here, lora, lora_got, out):
    in_pair = jnp.full((1, 1), where[IN_PAIR], jnp.int32) == 1
    base = one[...].astype(f32) + jnp.where(in_pair, here[...], two[...]).astype(f32)
    out[...] = (base + lora[...].astype(f32) + lora_got[...].astype(f32)).astype(bf16)


def pair_plan(
    activations,
    key_value_weight,
    token_adapter_index,
    adapter_down_weight,
    adapter_up_weight,
    cotangent,
):
    z = lax.axis_index("fsdp")
    y = lax.axis_index("groups")
    t = lax.axis_index("tp")
    x, c = t // 2, t % 2
    where = jnp.stack([y, z, x == z // 2, c == z % 2]).astype(jnp.int32)
    rows, width = key_value_weight.shape
    toks, out_width = cotangent.shape
    half, wide = rows // 2, width // 2
    down = adapter_down_weight[0]
    up = adapter_up_weight[0]
    rank = down.shape[0]
    places = [(zz, xx, cc) for zz in range(4) for xx in range(2) for cc in range(2)]

    cot_got = swap(cotangent, "fsdp", 2)
    idx_got = swap(token_adapter_index, "fsdp", 2)
    up_sib = swap(up, "fsdp", 1)
    w_mine = lax.dynamic_slice(key_value_weight, (0, y * wide), (rows, wide))
    d_mine = lax.dynamic_slice(down, (0, y * wide), (rank, wide))
    piece = jnp.concatenate([d_mine, w_mine[:half]], axis=0)
    near0 = swap(piece, "fsdp", 1)
    act_sent, _ = lax.optimization_barrier((activations, piece))
    act_got = swap(act_sent, "fsdp", 2)
    near1 = swap(w_mine[half:], "fsdp", 1)

    mine = local_kernel(
        back_kernel, ((2 * toks, out_width + 2 * rank), bf16), where,
        cotangent, cot_got, token_adapter_index, idx_got, up, up_sib,
    )
    mine = local_kernel(block_kernel, (mine.shape, bf16), where, mine, swap(mine, "tp", 2))
    got = swap(mine, "tp", 1)

    far0 = swap(near0, "groups", 1)
    far1 = swap(near1, "groups", 1)

    near, near_sent = gradient_half(where, y, mine, got, key_value_weight, down, near0, near1)
    near_got = swap(near_sent, "fsdp", 2)

    part = local_kernel(
        base_near_kernel, ((2 * toks, 2 * rows), f32), where,
        activations, act_got, key_value_weight, near0, near1,
    )

    low = local_kernel(
        low_kernel, ((2 * toks, 2 * rank), bf16), where,
        activations, act_got, token_adapter_index, idx_got, down, near0, far0,
    )
    low = (low.astype(f32) + swap(low, "tp", 2).astype(f32)).astype(bf16)
    low_got = swap(low, "tp", 1)

    far, far_sent = gradient_half(where, 1 - y, mine, got, key_value_weight, down, far0, far1)
    far_got = swap(far_sent, "fsdp", 2)

    keep, give = local_kernel(
        base_far_kernel, [((2 * toks, rows), f32), ((2 * toks, rows), bf16)], where,
        part, activations, act_got, far0, far1,
    )
    here, there, turn = local_kernel(
        held_kernel, [((toks, rows), bf16)] * 3, where, keep, swap(give, "tp", 1)
    )
    one = both(
        turn,
        [((a, b, d), (a ^ 2, b, d) if b == a // 2 else (a, 1 - b, d)) for a, b, d in places],
    )
    two = both(there, [((a, b, d), (a ^ 2, 1 - b, d)) for a, b, d in places if b != a // 2])

    lora, lora_far, down_own, up_own, sib = local_kernel(
        adapter_kernel,
        [
            ((toks, out_width), bf16),
            ((toks, out_width), bf16),
            ((rank, width), f32),
            ((rank, out_width), f32),
            ((rank, width + out_width), bf16),
        ],
        where,
        low, low_got, mine, got, activations, act_got, cotangent, cot_got, up, up_sib,
    )
    lora_got = swap(lora_far, "fsdp", 2)
    grad_down, up_gradient = local_kernel(
        adapter_end_kernel, [((1, rank, width), f32), ((1, rank, out_width), f32)], where,
        down_own, up_own, swap(sib, "fsdp", 1),
    )

    input_gradient = local_kernel(
        gradient_end_kernel, ((toks, width), bf16), where, near, near_got, far, far_got
    )
    key_value_output = local_kernel(
        output_kernel, ((toks, out_width), bf16), where, one, two, here, lora, lora_got
    )
    return (key_value_output, input_gradient, grad_down, up_gradient)


def solution(mesh):
    paired = mesh.shape["fsdp"] == 4 and mesh.shape["tp"] == 4 and mesh.shape["groups"] == 2
    return jax.shard_map(
        pair_plan if paired else gathered_plan,
        mesh=mesh,
        in_specs=(
            P(("groups", "fsdp"), "tp"),
            P("fsdp", "tp"),
            P(("groups", "fsdp"), None),
            P("fsdp", None, "tp"),
            P("fsdp", None, "tp"),
            P(("groups", "fsdp"), "tp"),
        ),
        out_specs=(
            P(("groups", "fsdp"), "tp"),
            P(("groups", "fsdp"), "tp"),
            P(("groups", "fsdp"), None, "tp"),
            P(("groups", "fsdp"), None, "tp"),
        ),
        check_vma=False,
    )
```

```python
import jax
import jax.numpy as jnp
from jax import lax
from jax.experimental import pallas as pl
from jax.experimental.pallas import tpu as pltpu
from jax.sharding import PartitionSpec as P

adapter_scale = 2.0
f32 = jnp.float32
bf16 = jnp.bfloat16


def placement_matrix(token_adapter_index, adapter_holders, slot_capacity):
    owner_of = token_adapter_index[:, 0]
    shard_member = (
        owner_of[:, None] == jnp.arange(adapter_holders, dtype=jnp.int32)[None, :]
    ).astype(jnp.int32)
    earlier = jnp.cumsum(shard_member, axis=0) - shard_member
    within = jnp.sum(earlier * shard_member, axis=1)
    target = owner_of * slot_capacity + within
    return (
        jnp.arange(adapter_holders * slot_capacity, dtype=jnp.int32)[:, None] == target[None, :]
    ).astype(jnp.bfloat16)


def pack_rows(placing, values, adapter_holders):
    packed = jnp.dot(placing, values, preferred_element_type=jnp.float32).astype(jnp.bfloat16)
    return packed.reshape(adapter_holders, -1, values.shape[1])


def unpack_rows(placing, returned):
    flat = returned.reshape(-1, returned.shape[2])
    return jnp.einsum("st,sk->tk", placing, flat, preferred_element_type=jnp.float32)


def gathered_plan(
    activations,
    key_value_weight,
    token_adapter_index,
    adapter_down_weight,
    adapter_up_weight,
    cotangent,
):
    adapter_holders = lax.axis_size("fsdp")
    tok_rows = activations.shape[0]
    slot_capacity = 2 * tok_rows // adapter_holders
    feature_width = activations.shape[1]
    output_width = cotangent.shape[1]
    placing = placement_matrix(token_adapter_index, adapter_holders, slot_capacity)
    down_resident = adapter_down_weight[0]
    up_resident = adapter_up_weight[0]
    whole_cot = lax.all_gather(cotangent, "tp", axis=1, tiled=True)
    whole_weight = lax.all_gather(key_value_weight, "fsdp", axis=0, tiled=True)
    partial_value = jnp.dot(activations, whole_weight.T, preferred_element_type=jnp.float32)
    base_gradient = jnp.dot(whole_cot, whole_weight, preferred_element_type=jnp.float32)
    base_output = lax.psum_scatter(
        partial_value.astype(jnp.bfloat16), "tp", scatter_dimension=1, tiled=True
    ).astype(jnp.float32)
    rows_send = pack_rows(placing, activations, adapter_holders)
    cot_send = pack_rows(placing, cotangent, adapter_holders)
    rows_recv = lax.all_to_all(rows_send, "fsdp", split_axis=0, concat_axis=0, tiled=True)
    rows_flat = rows_recv.reshape(-1, feature_width)
    low_part = jnp.dot(rows_flat, down_resident.T, preferred_element_type=jnp.float32)
    rank_activation = lax.psum(low_part.astype(jnp.bfloat16), "tp")
    adapter_output = (
        adapter_scale * jnp.dot(rank_activation, up_resident, preferred_element_type=jnp.float32)
    ).astype(jnp.bfloat16)
    out_back = lax.all_to_all(
        adapter_output.reshape(adapter_holders, slot_capacity, output_width),
        "fsdp",
        split_axis=0,
        concat_axis=0,
        tiled=True,
    )
    cot_recv = lax.all_to_all(cot_send, "fsdp", split_axis=0, concat_axis=0, tiled=True)
    flat_output_gradient = cot_recv.reshape(-1, output_width)
    backward_piece = adapter_scale * jnp.dot(
        flat_output_gradient, up_resident.T, preferred_element_type=jnp.float32
    )
    backward_result = lax.psum(backward_piece.astype(jnp.bfloat16), "tp")
    adapter_input = jnp.dot(
        backward_result, down_resident, preferred_element_type=jnp.float32
    ).astype(jnp.bfloat16)
    in_back = lax.all_to_all(
        adapter_input.reshape(adapter_holders, slot_capacity, feature_width),
        "fsdp",
        split_axis=0,
        concat_axis=0,
        tiled=True,
    )
    grad_down = jnp.einsum(
        "sr,sd->rd", backward_result, rows_flat, preferred_element_type=jnp.float32
    )
    up_gradient = adapter_scale * jnp.einsum(
        "sr,sk->rk", rank_activation, flat_output_gradient, preferred_element_type=jnp.float32
    )
    key_value_output = (base_output + unpack_rows(placing, out_back)).astype(jnp.bfloat16)
    input_gradient = (base_gradient + unpack_rows(placing, in_back)).astype(jnp.bfloat16)
    return (key_value_output, input_gradient, grad_down[None], up_gradient[None])


def nn(a, b):
    return lax.dot_general(a, b, (((1,), (0,)), ((), ())), preferred_element_type=f32)


def nt(a, b):
    return lax.dot_general(a, b, (((1,), (1,)), ((), ())), preferred_element_type=f32)


def tn(a, b):
    return lax.dot_general(a, b, (((0,), (0,)), ((), ())), preferred_element_type=f32)


def rows2(a, b):
    return jnp.concatenate([a, b], axis=0)


def swap(x, axis, bit):
    return lax.ppermute(x, axis, [(i, i ^ bit) for i in range(lax.axis_size(axis))])


def both(x, pairs):
    flat = [(4 * a[0] + 2 * a[1] + a[2], 4 * b[0] + 2 * b[1] + b[2]) for a, b in pairs]
    return lax.ppermute(x, ("fsdp", "tp"), flat)


def after(values, *earlier):
    return lax.optimization_barrier((values, earlier))[0]


Y, Z, IN_PAIR, ON_OWN = range(4)


def cost(us):
    return pl.CostEstimate(flops=0, bytes_accessed=1000 + us * 3_000_000, transcendentals=0)


def local_kernel(body, outs, where, *args, us=0):
    single = not isinstance(outs, list)
    shapes = [jax.ShapeDtypeStruct(s, d) for s, d in ([outs] if single else outs)]
    got = pl.pallas_call(
        body,
        out_shape=shapes,
        in_specs=[pl.BlockSpec(memory_space=pltpu.SMEM)]
        + [pl.BlockSpec(memory_space=pltpu.VMEM)] * len(args),
        out_specs=[pl.BlockSpec(memory_space=pltpu.VMEM)] * len(shapes),
        compiler_params=pltpu.CompilerParams(vmem_limit_bytes=12 * 1024 * 1024),
        cost_estimate=cost(us),
    )(where, *args)
    return got[0] if single else got


def member(where, idx, rank):
    lane = lax.broadcasted_iota(jnp.int32, (idx.shape[0], 2 * rank), 1)
    z = where[Z]
    return idx == jnp.where(lane < rank, z, z ^ 1)


def column(row):
    n = row.shape[1]
    same = lax.broadcasted_iota(jnp.int32, (n, n), 0) == lax.broadcasted_iota(jnp.int32, (n, n), 1)
    picked = jnp.where(same, jnp.broadcast_to(row, (n, n)).astype(f32), 0.0)
    return jnp.sum(picked, axis=1, keepdims=True).astype(jnp.int32)


def back_kernel(where, cot, cot_got, idx, up, up_sib, out, members):
    width = cot.shape[1]
    toks = cot.shape[0]
    cot2 = rows2(cot[...], cot_got[:toks, :])
    part = adapter_scale * nt(cot2, rows2(up[...], up_sib[...]))
    idx_got = cot_got[toks:, :toks].astype(f32)[:1].astype(jnp.int32)
    mine = member(where, rows2(column(idx[...]), column(idx_got)), up.shape[0])
    members[...] = mine.astype(bf16)
    out[:, :width] = cot2
    out[:, width:] = jnp.where(mine, part, 0.0).astype(bf16)


def block_kernel(where, mine, got, out):
    width = out.shape[1] - 128
    in_pair = jnp.full((1, 1), where[IN_PAIR], jnp.int32) == 1
    out[:, :width] = jnp.where(in_pair, mine[:, :width], got[:, :width])
    out[:, width:] = (mine[:, width:].astype(f32) + got[:, width:].astype(f32)).astype(bf16)


def pair_blocks(where, mine, got):
    width = mine.shape[1] - 128
    on_own = jnp.full((1, 1), where[ON_OWN], jnp.int32) == 1
    a, b = mine[:, :width], got[:, :width]
    return jnp.where(on_own, a, b), jnp.where(on_own, b, a)


def whole_back(mine, got):
    width = mine.shape[1] - 128
    return (mine[:, width:].astype(f32) + got[:, width:].astype(f32)).astype(bf16)


def gradient_kernel(where, mine, got, weight, down, first, second, top, bottom):
    rank = down.shape[0]
    head = first.shape[0] - rank
    c_own, c_sib = pair_blocks(where, mine, got)
    back = whole_back(mine, got)
    g = nn(c_own, weight[...])
    g += nn(c_sib[:, :head], first[rank:, :])
    g += nn(c_sib[:, head:], second[...])
    g += nn(back, rows2(down[...], first[:rank, :]))
    toks = top.shape[0]
    top[...] = g[:toks]
    bottom[...] = g[toks:].astype(bf16)


def gradient_half(where, side, mine, got, weight, down, first, second):
    toks, tile = mine.shape[0] // 2, 512
    steps = first.shape[1] // tile
    whole = lambda a: pl.BlockSpec(a.shape, lambda j, s: (0, 0))
    by_side = lambda a: pl.BlockSpec((a.shape[0], tile), lambda j, s: (0, s[4] * steps + j))
    tiled = lambda n: pl.BlockSpec((n, tile), lambda j, s: (0, j))
    return pl.pallas_call(
        gradient_kernel,
        grid_spec=pltpu.PrefetchScalarGridSpec(
            num_scalar_prefetch=1,
            grid=(steps,),
            in_specs=[
                whole(mine),
                whole(got),
                by_side(weight),
                by_side(down),
                tiled(first.shape[0]),
                tiled(second.shape[0]),
            ],
            out_specs=[tiled(toks), tiled(toks)],
        ),
        out_shape=[
            jax.ShapeDtypeStruct((toks, steps * tile), f32),
            jax.ShapeDtypeStruct((toks, steps * tile), bf16),
        ],
        compiler_params=pltpu.CompilerParams(vmem_limit_bytes=12 * 1024 * 1024),
        cost_estimate=cost(0),
    )(jnp.concatenate([where, side[None]]), mine, got, weight, down, first, second)


def gradient_end_kernel(where, near, near_got, far, far_got, out):
    half = near.shape[1]
    y = where[Y]
    at = pl.ds(pl.multiple_of(y * half, half), half)
    out[:, at] = (near[...] + near_got[...].astype(f32)).astype(bf16)
    at = pl.ds(pl.multiple_of((1 - y) * half, half), half)
    out[:, at] = (far[...] + far_got[...].astype(f32)).astype(bf16)


def low_kernel(where, act, act_got, members, down, near, far, out):
    rank, half = down.shape[0], near.shape[1]
    y = where[Y]
    at_near = pl.ds(pl.multiple_of(y * half, half), half)
    at_far = pl.ds(pl.multiple_of((1 - y) * half, half), half)
    part = nt(rows2(act[:, at_near], act_got[:, at_near]), rows2(down[:, at_near], near[:rank, :]))
    part += nt(rows2(act[:, at_far], act_got[:, at_far]), rows2(down[:, at_far], far[:rank, :]))
    out[...] = jnp.where(members[...] != 0, part, 0.0).astype(bf16)


def adapter_kernel(
    where, give, give_got, mine, got, act, act_got, cot, cot_got, up, up_sib,
    lora, lora_far, down_own, up_own, sib,
):
    rank, width, toks = up.shape[0], act.shape[1], act.shape[0]
    whole_low = whole_back(give, give_got)
    out = (adapter_scale * nn(whole_low, rows2(up[...], up_sib[...]))).astype(bf16)
    lora[...] = out[:toks]
    lora_far[...] = out[toks:]
    grad = tn(whole_back(mine, got), rows2(act[...], act_got[...]))
    down_own[...] = grad[:rank]
    sib[:, :width] = grad[rank:].astype(bf16)
    grad = adapter_scale * tn(whole_low, rows2(cot[...], cot_got[: cot.shape[0], :]))
    up_own[...] = grad[:rank]
    sib[:, width:] = grad[rank:].astype(bf16)


def adapter_end_kernel(where, down_own, up_own, got, down_out, up_out):
    width = down_own.shape[1]
    down_out[0] = down_own[...] + got[:, :width].astype(f32)
    up_out[0] = up_own[...] + got[:, width:].astype(f32)


def base_near_kernel(where, act, act_got, weight, first, second, out):
    rows = weight.shape[0]
    head = rows - second.shape[0]
    cut = first.shape[0] - head
    wide = first.shape[1]
    at = pl.ds(pl.multiple_of(where[Y] * wide, wide), wide)
    near = rows2(act[:, at], act_got[:, at])
    out[:, :rows] = nt(rows2(act[...], act_got[...]), weight[...])
    out[:, rows : rows + head] = nt(near, first[cut:, :])
    out[:, rows + head :] = nt(near, second[...])


def base_far_kernel(where, part, act, act_got, first, second, low, low_got, keep, give):
    rows = keep.shape[1]
    head = rows - second.shape[0]
    cut = first.shape[0] - head
    wide = first.shape[1]
    at = pl.ds(pl.multiple_of((1 - where[Y]) * wide, wide), wide)
    far = rows2(act[:, at], act_got[:, at])
    on_own = jnp.full((1, 1), where[ON_OWN], jnp.int32) == 1
    for lo, hi, block in ((0, head, first[cut:, :]), (head, rows, second[...])):
        mine = part[:, lo:hi]
        other = part[:, rows + lo : rows + hi] + nt(far, block)
        keep[:, lo:hi] = jnp.where(on_own, mine, other)
        give[:, lo:hi] = jnp.where(on_own, other, mine).astype(bf16)
    give[:, rows:] = (low[...].astype(f32) + low_got[...].astype(f32)).astype(bf16)


def held_kernel(where, keep, got, here, there, turn):
    toks, rows = here.shape
    held = (keep[...] + got[:, :rows].astype(f32)).astype(bf16)
    in_pair = jnp.full((1, 1), where[IN_PAIR], jnp.int32) == 1
    here[...] = held[:toks]
    there[...] = held[toks:]
    turn[...] = jnp.where(in_pair, held[toks:], held[:toks])


def output_kernel(where, one, two, here, lora, lora_got, out):
    in_pair = jnp.full((1, 1), where[IN_PAIR], jnp.int32) == 1
    base = one[...].astype(f32) + jnp.where(in_pair, here[...], two[...]).astype(f32)
    out[...] = (base + lora[...].astype(f32) + lora_got[...].astype(f32)).astype(bf16)


def pair_plan(
    activations,
    key_value_weight,
    token_adapter_index,
    adapter_down_weight,
    adapter_up_weight,
    cotangent,
):
    z = lax.axis_index("fsdp")
    y = lax.axis_index("groups")
    t = lax.axis_index("tp")
    x, c = t // 2, t % 2
    where = jnp.stack([y, z, x == z // 2, c == z % 2]).astype(jnp.int32)
    rows, width = key_value_weight.shape
    toks, out_width = cotangent.shape
    half, wide = rows // 2, width // 2
    down = adapter_down_weight[0]
    up = adapter_up_weight[0]
    rank = down.shape[0]
    places = [(zz, xx, cc) for zz in range(4) for xx in range(2) for cc in range(2)]

    idx = token_adapter_index.reshape(1, toks)
    idx_row = jnp.pad(idx.astype(bf16), ((0, 15), (0, out_width - toks)))
    cot_got = swap(jnp.concatenate([cotangent, idx_row], axis=0), "fsdp", 2)
    up_sib = swap(up, "fsdp", 1)
    w_mine = lax.dynamic_slice(key_value_weight, (0, y * wide), (rows, wide))
    d_mine = lax.dynamic_slice(down, (0, y * wide), (rank, wide))
    head = rows * 2 // 4
    piece0 = jnp.concatenate([d_mine, w_mine[:head]], axis=0)
    piece1 = w_mine[head:]
    piece0, piece1 = after((piece0, piece1), cot_got, up_sib)
    near0 = swap(piece0, "fsdp", 1)
    near1 = swap(piece1, "fsdp", 1)

    mine, members = local_kernel(
        back_kernel,
        [((2 * toks, out_width + 2 * rank), bf16), ((2 * toks, 2 * rank), bf16)],
        where,
        cotangent, cot_got, idx, up, up_sib, us=20,
    )
    mine_x = swap(mine, "tp", 2)
    act_got = swap(after(activations, mine), "fsdp", 2)
    near0 = after(near0, mine)
    far0 = swap(near0, "groups", 1)
    far1 = swap(near1, "groups", 1)
    mine_x = after(mine_x, near1)
    mine = local_kernel(block_kernel, (mine.shape, bf16), where, mine, mine_x)
    got = swap(mine, "tp", 1)

    near, near_sent = gradient_half(where, y, mine, got, key_value_weight, down, near0, near1)
    near_got = swap(near_sent, "fsdp", 2)

    act_got = after(act_got, near_sent)
    part = local_kernel(
        base_near_kernel, ((2 * toks, 2 * rows), f32), where,
        activations, act_got, key_value_weight, near0, near1, us=15,
    )

    far0 = after(far0, part)
    low = local_kernel(
        low_kernel, ((2 * toks, 2 * rank), bf16), where,
        activations, act_got, members, down, near0, far0,
    )
    low_x = swap(low, "tp", 2)

    far1 = after(far1, low)
    far, far_sent = gradient_half(where, 1 - y, mine, got, key_value_weight, down, far0, far1)
    far_got = swap(far_sent, "fsdp", 2)

    part, near_got = after((part, near_got), far_sent)
    keep, give = local_kernel(
        base_far_kernel,
        [((2 * toks, rows), f32), ((2 * toks, rows + 2 * rank), bf16)],
        where,
        part, activations, act_got, far0, far1, low, low_x, us=10,
    )
    give_got = swap(give, "tp", 1)
    here, there, turn = local_kernel(
        held_kernel, [((toks, rows), bf16)] * 3, where, keep, give_got
    )
    one = both(
        turn,
        [((a, b, d), (a ^ 2, b, d) if b == a // 2 else (a, 1 - b, d)) for a, b, d in places],
    )
    two = both(there, [((a, b, d), (a ^ 2, 1 - b, d)) for a, b, d in places if b != a // 2])

    give_got = after(give_got, here)
    lora, lora_far, down_own, up_own, sib = local_kernel(
        adapter_kernel,
        [
            ((toks, out_width), bf16),
            ((toks, out_width), bf16),
            ((rank, width), f32),
            ((rank, out_width), f32),
            ((rank, width + out_width), bf16),
        ],
        where,
        give, give_got, mine, got, activations, act_got, cotangent, cot_got, up, up_sib, us=5,
    )
    lora_got = swap(lora_far, "fsdp", 2)
    grad_down, up_gradient = local_kernel(
        adapter_end_kernel, [((1, rank, width), f32), ((1, rank, out_width), f32)], where,
        down_own, up_own, swap(sib, "fsdp", 1),
    )

    input_gradient = local_kernel(
        gradient_end_kernel, ((toks, width), bf16), where, near, near_got, far, far_got
    )
    key_value_output = local_kernel(
        output_kernel, ((toks, out_width), bf16), where, one, two, here, lora, lora_got
    )
    return (key_value_output, input_gradient, grad_down, up_gradient)


def solution(mesh):
    paired = mesh.shape["fsdp"] == 4 and mesh.shape["tp"] == 4 and mesh.shape["groups"] == 2
    return jax.shard_map(
        pair_plan if paired else gathered_plan,
        mesh=mesh,
        in_specs=(
            P(("groups", "fsdp"), "tp"),
            P("fsdp", "tp"),
            P(("groups", "fsdp"), None),
            P("fsdp", None, "tp"),
            P("fsdp", None, "tp"),
            P(("groups", "fsdp"), "tp"),
        ),
        out_specs=(
            P(("groups", "fsdp"), "tp"),
            P(("groups", "fsdp"), "tp"),
            P(("groups", "fsdp"), None, "tp"),
            P(("groups", "fsdp"), None, "tp"),
        ),
        check_vma=False,
    )
```

```python
import jax
import jax.numpy as jnp
from jax import lax
from jax.experimental import pallas as pl
from jax.experimental.pallas import tpu as pltpu
from jax.sharding import PartitionSpec as P

adapter_scale = 2.0
f32 = jnp.float32
bf16 = jnp.bfloat16


def placement_matrix(token_adapter_index, adapter_holders, slot_capacity):
    owner_of = token_adapter_index[:, 0]
    shard_member = (
        owner_of[:, None] == jnp.arange(adapter_holders, dtype=jnp.int32)[None, :]
    ).astype(jnp.int32)
    earlier = jnp.cumsum(shard_member, axis=0) - shard_member
    within = jnp.sum(earlier * shard_member, axis=1)
    target = owner_of * slot_capacity + within
    return (
        jnp.arange(adapter_holders * slot_capacity, dtype=jnp.int32)[:, None] == target[None, :]
    ).astype(jnp.bfloat16)


def pack_rows(placing, values, adapter_holders):
    packed = jnp.dot(placing, values, preferred_element_type=jnp.float32).astype(jnp.bfloat16)
    return packed.reshape(adapter_holders, -1, values.shape[1])


def unpack_rows(placing, returned):
    flat = returned.reshape(-1, returned.shape[2])
    return jnp.einsum("st,sk->tk", placing, flat, preferred_element_type=jnp.float32)


def gathered_plan(
    activations,
    key_value_weight,
    token_adapter_index,
    adapter_down_weight,
    adapter_up_weight,
    cotangent,
):
    adapter_holders = lax.axis_size("fsdp")
    tok_rows = activations.shape[0]
    slot_capacity = 2 * tok_rows // adapter_holders
    feature_width = activations.shape[1]
    output_width = cotangent.shape[1]
    placing = placement_matrix(token_adapter_index, adapter_holders, slot_capacity)
    down_resident = adapter_down_weight[0]
    up_resident = adapter_up_weight[0]
    whole_cot = lax.all_gather(cotangent, "tp", axis=1, tiled=True)
    whole_weight = lax.all_gather(key_value_weight, "fsdp", axis=0, tiled=True)
    partial_value = jnp.dot(activations, whole_weight.T, preferred_element_type=jnp.float32)
    base_gradient = jnp.dot(whole_cot, whole_weight, preferred_element_type=jnp.float32)
    base_output = lax.psum_scatter(
        partial_value.astype(jnp.bfloat16), "tp", scatter_dimension=1, tiled=True
    ).astype(jnp.float32)
    rows_send = pack_rows(placing, activations, adapter_holders)
    cot_send = pack_rows(placing, cotangent, adapter_holders)
    rows_recv = lax.all_to_all(rows_send, "fsdp", split_axis=0, concat_axis=0, tiled=True)
    rows_flat = rows_recv.reshape(-1, feature_width)
    low_part = jnp.dot(rows_flat, down_resident.T, preferred_element_type=jnp.float32)
    rank_activation = lax.psum(low_part.astype(jnp.bfloat16), "tp")
    adapter_output = (
        adapter_scale * jnp.dot(rank_activation, up_resident, preferred_element_type=jnp.float32)
    ).astype(jnp.bfloat16)
    out_back = lax.all_to_all(
        adapter_output.reshape(adapter_holders, slot_capacity, output_width),
        "fsdp",
        split_axis=0,
        concat_axis=0,
        tiled=True,
    )
    cot_recv = lax.all_to_all(cot_send, "fsdp", split_axis=0, concat_axis=0, tiled=True)
    flat_output_gradient = cot_recv.reshape(-1, output_width)
    backward_piece = adapter_scale * jnp.dot(
        flat_output_gradient, up_resident.T, preferred_element_type=jnp.float32
    )
    backward_result = lax.psum(backward_piece.astype(jnp.bfloat16), "tp")
    adapter_input = jnp.dot(
        backward_result, down_resident, preferred_element_type=jnp.float32
    ).astype(jnp.bfloat16)
    in_back = lax.all_to_all(
        adapter_input.reshape(adapter_holders, slot_capacity, feature_width),
        "fsdp",
        split_axis=0,
        concat_axis=0,
        tiled=True,
    )
    grad_down = jnp.einsum(
        "sr,sd->rd", backward_result, rows_flat, preferred_element_type=jnp.float32
    )
    up_gradient = adapter_scale * jnp.einsum(
        "sr,sk->rk", rank_activation, flat_output_gradient, preferred_element_type=jnp.float32
    )
    key_value_output = (base_output + unpack_rows(placing, out_back)).astype(jnp.bfloat16)
    input_gradient = (base_gradient + unpack_rows(placing, in_back)).astype(jnp.bfloat16)
    return (key_value_output, input_gradient, grad_down[None], up_gradient[None])


def nn(a, b):
    return lax.dot_general(a, b, (((1,), (0,)), ((), ())), preferred_element_type=f32)


def nt(a, b):
    return lax.dot_general(a, b, (((1,), (1,)), ((), ())), preferred_element_type=f32)


def tn(a, b):
    return lax.dot_general(a, b, (((0,), (0,)), ((), ())), preferred_element_type=f32)


def rows2(a, b):
    return jnp.concatenate([a, b], axis=0)


def swap(x, axis, bit):
    return lax.ppermute(x, axis, [(i, i ^ bit) for i in range(lax.axis_size(axis))])


def both(x, pairs):
    flat = [(4 * a[0] + 2 * a[1] + a[2], 4 * b[0] + 2 * b[1] + b[2]) for a, b in pairs]
    return lax.ppermute(x, ("fsdp", "tp"), flat)


def after(values, *earlier):
    return lax.optimization_barrier((values, earlier))[0]


Y, Z, IN_PAIR, ON_OWN = range(4)


def cost(us):
    return pl.CostEstimate(flops=us * 1_000_000_000, bytes_accessed=1000 + us * 3_000_000, transcendentals=0)


def local_kernel(body, outs, where, *args, us=0):
    single = not isinstance(outs, list)
    shapes = [jax.ShapeDtypeStruct(s, d) for s, d in ([outs] if single else outs)]
    got = pl.pallas_call(
        body,
        out_shape=shapes,
        in_specs=[pl.BlockSpec(memory_space=pltpu.SMEM)]
        + [pl.BlockSpec(memory_space=pltpu.VMEM)] * len(args),
        out_specs=[pl.BlockSpec(memory_space=pltpu.VMEM)] * len(shapes),
        compiler_params=pltpu.CompilerParams(vmem_limit_bytes=12 * 1024 * 1024),
        cost_estimate=cost(us),
    )(where, *args)
    return got[0] if single else got


def member(where, idx, rank):
    lane = lax.broadcasted_iota(jnp.int32, (idx.shape[0], 2 * rank), 1)
    z = where[Z]
    return idx == jnp.where(lane < rank, z, z ^ 1)


def column(row):
    n = row.shape[1]
    same = lax.broadcasted_iota(jnp.int32, (n, n), 0) == lax.broadcasted_iota(jnp.int32, (n, n), 1)
    picked = jnp.where(same, jnp.broadcast_to(row, (n, n)).astype(f32), 0.0)
    return jnp.sum(picked, axis=1, keepdims=True).astype(jnp.int32)


def back_kernel(where, cot, cot_got, idx, up, up_sib, out, members):
    width = cot.shape[1]
    toks = cot.shape[0]
    cot2 = rows2(cot[...], cot_got[:toks, :])
    part = adapter_scale * nt(cot2, rows2(up[...], up_sib[...]))
    idx_got = cot_got[toks:, :toks].astype(f32)[:1].astype(jnp.int32)
    mine = member(where, rows2(column(idx[...]), column(idx_got)), up.shape[0])
    members[...] = mine.astype(bf16)
    out[:, :width] = cot2
    out[:, width:] = jnp.where(mine, part, 0.0).astype(bf16)


def block_kernel(where, mine, got, out):
    width = out.shape[1] - 128
    in_pair = jnp.full((1, 1), where[IN_PAIR], jnp.int32) == 1
    out[:, :width] = jnp.where(in_pair, mine[:, :width], got[:, :width])
    out[:, width:] = (mine[:, width:].astype(f32) + got[:, width:].astype(f32)).astype(bf16)


def pair_blocks(where, mine, got):
    width = mine.shape[1] - 128
    on_own = jnp.full((1, 1), where[ON_OWN], jnp.int32) == 1
    a, b = mine[:, :width], got[:, :width]
    return jnp.where(on_own, a, b), jnp.where(on_own, b, a)


def whole_back(mine, got):
    width = mine.shape[1] - 128
    return (mine[:, width:].astype(f32) + got[:, width:].astype(f32)).astype(bf16)


def gradient_kernel(where, mine, got, weight, down, first, second, top, bottom):
    rank = down.shape[0]
    head = first.shape[0] - rank
    c_own, c_sib = pair_blocks(where, mine, got)
    back = whole_back(mine, got)
    g = nn(c_own, weight[...])
    g += nn(c_sib[:, :head], first[rank:, :])
    g += nn(c_sib[:, head:], second[...])
    g += nn(back, rows2(down[...], first[:rank, :]))
    toks = top.shape[0]
    top[...] = g[:toks].astype(bf16)
    bottom[...] = g[toks:].astype(bf16)


def gradient_half(where, side, mine, got, weight, down, first, second):
    toks, tile = mine.shape[0] // 2, 512
    steps = first.shape[1] // tile
    whole = lambda a: pl.BlockSpec(a.shape, lambda j, s: (0, 0))
    by_side = lambda a: pl.BlockSpec((a.shape[0], tile), lambda j, s: (0, s[4] * steps + j))
    tiled = lambda n: pl.BlockSpec((n, tile), lambda j, s: (0, j))
    return pl.pallas_call(
        gradient_kernel,
        grid_spec=pltpu.PrefetchScalarGridSpec(
            num_scalar_prefetch=1,
            grid=(steps,),
            in_specs=[
                whole(mine),
                whole(got),
                by_side(weight),
                by_side(down),
                tiled(first.shape[0]),
                tiled(second.shape[0]),
            ],
            out_specs=[tiled(toks), tiled(toks)],
        ),
        out_shape=[
            jax.ShapeDtypeStruct((toks, steps * tile), bf16),
            jax.ShapeDtypeStruct((toks, steps * tile), bf16),
        ],
        compiler_params=pltpu.CompilerParams(vmem_limit_bytes=12 * 1024 * 1024),
        cost_estimate=cost(0),
    )(jnp.concatenate([where, side[None]]), mine, got, weight, down, first, second)


def gradient_end_kernel(where, near, near_got, far, far_got, out):
    half = near.shape[1]
    y = where[Y]
    at = pl.ds(pl.multiple_of(y * half, half), half)
    out[:, at] = (near[...].astype(f32) + near_got[...].astype(f32)).astype(bf16)
    at = pl.ds(pl.multiple_of((1 - y) * half, half), half)
    out[:, at] = (far[...].astype(f32) + far_got[...].astype(f32)).astype(bf16)


def low_kernel(where, act, act_got, members, down, near, far, out):
    rank, half = down.shape[0], near.shape[1]
    y = where[Y]
    at_near = pl.ds(pl.multiple_of(y * half, half), half)
    at_far = pl.ds(pl.multiple_of((1 - y) * half, half), half)
    part = nt(rows2(act[:, at_near], act_got[:, at_near]), rows2(down[:, at_near], near[:rank, :]))
    part += nt(rows2(act[:, at_far], act_got[:, at_far]), rows2(down[:, at_far], far[:rank, :]))
    out[...] = jnp.where(members[...] != 0, part, 0.0).astype(bf16)


def adapter_kernel(
    where, give, give_got, mine, got, act, act_got, cot, cot_got, up, up_sib,
    lora, lora_far, down_own, up_own, sib,
):
    rank, width, toks = up.shape[0], act.shape[1], act.shape[0]
    whole_low = whole_back(give, give_got)
    out = (adapter_scale * nn(whole_low, rows2(up[...], up_sib[...]))).astype(bf16)
    lora[...] = out[:toks]
    lora_far[...] = out[toks:]
    grad = tn(whole_back(mine, got), rows2(act[...], act_got[...]))
    down_own[...] = grad[:rank]
    sib[:, :width] = grad[rank:].astype(bf16)
    grad = adapter_scale * tn(whole_low, rows2(cot[...], cot_got[: cot.shape[0], :]))
    up_own[...] = grad[:rank]
    sib[:, width:] = grad[rank:].astype(bf16)


def adapter_end_kernel(where, down_own, up_own, got, down_out, up_out):
    width = down_own.shape[1]
    down_out[0] = down_own[...] + got[:, :width].astype(f32)
    up_out[0] = up_own[...] + got[:, width:].astype(f32)


def base_near_kernel(where, act, act_got, weight, first, second, out):
    rows = weight.shape[0]
    head = rows - second.shape[0]
    cut = first.shape[0] - head
    wide = first.shape[1]
    at = pl.ds(pl.multiple_of(where[Y] * wide, wide), wide)
    near = rows2(act[:, at], act_got[:, at])
    out[:, :rows] = nt(rows2(act[...], act_got[...]), weight[...])
    out[:, rows : rows + head] = nt(near, first[cut:, :])
    out[:, rows + head :] = nt(near, second[...])


def base_far_kernel(where, part, act, act_got, first, second, low, low_got, keep, give):
    rows = keep.shape[1]
    head = rows - second.shape[0]
    cut = first.shape[0] - head
    wide = first.shape[1]
    at = pl.ds(pl.multiple_of((1 - where[Y]) * wide, wide), wide)
    far = rows2(act[:, at], act_got[:, at])
    on_own = jnp.full((1, 1), where[ON_OWN], jnp.int32) == 1
    for lo, hi, block in ((0, head, first[cut:, :]), (head, rows, second[...])):
        mine = part[:, lo:hi]
        other = part[:, rows + lo : rows + hi] + nt(far, block)
        keep[:, lo:hi] = jnp.where(on_own, mine, other)
        give[:, lo:hi] = jnp.where(on_own, other, mine).astype(bf16)
    give[:, rows:] = (low[...].astype(f32) + low_got[...].astype(f32)).astype(bf16)


def held_kernel(where, keep, got, held):
    held[...] = (keep[...] + got[:, : keep.shape[1]].astype(f32)).astype(bf16)


def turn_kernel(where, held, got, lora_far, turn):
    toks = turn.shape[0]
    in_pair = jnp.full((1, 1), where[IN_PAIR], jnp.int32) == 1
    base = held[toks:, :].astype(f32) + got[toks:, :].astype(f32)
    turn[...] = (lora_far[...].astype(f32) + jnp.where(in_pair, base, 0.0)).astype(bf16)


def output_kernel(where, held, got, lora, turned, out):
    toks = out.shape[0]
    in_pair = jnp.full((1, 1), where[IN_PAIR], jnp.int32) == 1
    base = held[:toks, :].astype(f32) + got[:toks, :].astype(f32)
    total = turned[...].astype(f32) + jnp.where(in_pair, base, 0.0)
    out[...] = (total + lora[...].astype(f32)).astype(bf16)


def pair_plan(
    activations,
    key_value_weight,
    token_adapter_index,
    adapter_down_weight,
    adapter_up_weight,
    cotangent,
):
    z = lax.axis_index("fsdp")
    y = lax.axis_index("groups")
    t = lax.axis_index("tp")
    x, c = t // 2, t % 2
    where = jnp.stack([y, z, x == z // 2, c == z % 2]).astype(jnp.int32)
    rows, width = key_value_weight.shape
    toks, out_width = cotangent.shape
    half, wide = rows // 2, width // 2
    down = adapter_down_weight[0]
    up = adapter_up_weight[0]
    rank = down.shape[0]
    places = [(zz, xx, cc) for zz in range(4) for xx in range(2) for cc in range(2)]

    idx = token_adapter_index.reshape(1, toks)
    idx_row = jnp.pad(idx.astype(bf16), ((0, 15), (0, out_width - toks)))
    cot_got = swap(jnp.concatenate([cotangent, idx_row], axis=0), "fsdp", 2)
    up_sib = swap(up, "fsdp", 1)
    w_mine = lax.dynamic_slice(key_value_weight, (0, y * wide), (rows, wide))
    d_mine = lax.dynamic_slice(down, (0, y * wide), (rank, wide))
    head = rows * 2 // 4
    piece0 = jnp.concatenate([d_mine, w_mine[:head]], axis=0)
    piece1 = w_mine[head:]
    near0 = swap(piece0, "fsdp", 1)
    act_got = swap(after(activations, cot_got, up_sib), "fsdp", 2)
    near1 = swap(after(piece1, cot_got, up_sib), "fsdp", 1)

    mine, members = local_kernel(
        back_kernel,
        [((2 * toks, out_width + 2 * rank), bf16), ((2 * toks, 2 * rank), bf16)],
        where,
        cotangent, cot_got, idx, up, up_sib, us=0,
    )
    mine_x = swap(mine, "tp", 2)
    near0 = after(near0, mine)
    far0 = swap(near0, "groups", 1)
    far1 = swap(near1, "groups", 1)
    mine_x = after(mine_x, near1)
    mine = local_kernel(block_kernel, (mine.shape, bf16), where, mine, mine_x)
    got = swap(mine, "tp", 1)

    near, near_sent = gradient_half(where, y, mine, got, key_value_weight, down, near0, near1)
    near_got = swap(near_sent, "fsdp", 2)

    act_got = after(act_got, near_sent)
    part = local_kernel(
        base_near_kernel, ((2 * toks, 2 * rows), f32), where,
        activations, act_got, key_value_weight, near0, near1, us=0,
    )

    far0 = after(far0, part)
    low = local_kernel(
        low_kernel, ((2 * toks, 2 * rank), bf16), where,
        activations, act_got, members, down, near0, far0,
    )
    low_x = swap(low, "tp", 2)

    far1 = after(far1, low)
    far, far_sent = gradient_half(where, 1 - y, mine, got, key_value_weight, down, far0, far1)
    far_got = swap(far_sent, "fsdp", 2)

    part, near_got = after((part, near_got), far_sent)
    keep, give = local_kernel(
        base_far_kernel,
        [((2 * toks, rows), f32), ((2 * toks, rows + 2 * rank), bf16)],
        where,
        part, activations, act_got, far0, far1, low, low_x, us=0,
    )
    give_got = swap(give, "tp", 1)
    held = local_kernel(held_kernel, ((2 * toks, rows), bf16), where, keep, give_got)
    held_got = both(held, [((a, b, d), (a, 1 - b, d)) for a, b, d in places if b != a // 2])

    give_got = after(give_got, held)
    lora, lora_far, down_own, up_own, sib = local_kernel(
        adapter_kernel,
        [
            ((toks, out_width), bf16),
            ((toks, out_width), bf16),
            ((rank, width), f32),
            ((rank, out_width), f32),
            ((rank, width + out_width), bf16),
        ],
        where,
        give, give_got, mine, got, activations, act_got, cotangent, cot_got, up, up_sib, us=0,
    )
    turn = local_kernel(
        turn_kernel, ((toks, out_width), bf16), where, held, held_got, lora_far
    )
    turned = swap(turn, "fsdp", 2)
    grad_down, up_gradient = local_kernel(
        adapter_end_kernel, [((1, rank, width), f32), ((1, rank, out_width), f32)], where,
        down_own, up_own, swap(sib, "fsdp", 1),
    )

    input_gradient = local_kernel(
        gradient_end_kernel, ((toks, width), bf16), where, near, near_got, far, far_got
    )
    key_value_output = local_kernel(
        output_kernel, ((toks, out_width), bf16), where, held, held_got, lora, turned
    )
    return (key_value_output, input_gradient, grad_down, up_gradient)


def solution(mesh):
    paired = mesh.shape["fsdp"] == 4 and mesh.shape["tp"] == 4 and mesh.shape["groups"] == 2
    return jax.shard_map(
        pair_plan if paired else gathered_plan,
        mesh=mesh,
        in_specs=(
            P(("groups", "fsdp"), "tp"),
            P("fsdp", "tp"),
            P(("groups", "fsdp"), None),
            P("fsdp", None, "tp"),
            P("fsdp", None, "tp"),
            P(("groups", "fsdp"), "tp"),
        ),
        out_specs=(
            P(("groups", "fsdp"), "tp"),
            P(("groups", "fsdp"), "tp"),
            P(("groups", "fsdp"), None, "tp"),
            P(("groups", "fsdp"), None, "tp"),
        ),
        check_vma=False,
    )
```

```python
import jax
import jax.numpy as jnp
from jax import lax
from jax.experimental import pallas as pl
from jax.experimental.pallas import tpu as pltpu
from jax.sharding import PartitionSpec as P

adapter_scale = 2.0
f32 = jnp.float32
bf16 = jnp.bfloat16


def placement_matrix(token_adapter_index, adapter_holders, slot_capacity):
    owner_of = token_adapter_index[:, 0]
    shard_member = (
        owner_of[:, None] == jnp.arange(adapter_holders, dtype=jnp.int32)[None, :]
    ).astype(jnp.int32)
    earlier = jnp.cumsum(shard_member, axis=0) - shard_member
    within = jnp.sum(earlier * shard_member, axis=1)
    target = owner_of * slot_capacity + within
    return (
        jnp.arange(adapter_holders * slot_capacity, dtype=jnp.int32)[:, None] == target[None, :]
    ).astype(jnp.bfloat16)


def pack_rows(placing, values, adapter_holders):
    packed = jnp.dot(placing, values, preferred_element_type=jnp.float32).astype(jnp.bfloat16)
    return packed.reshape(adapter_holders, -1, values.shape[1])


def unpack_rows(placing, returned):
    flat = returned.reshape(-1, returned.shape[2])
    return jnp.einsum("st,sk->tk", placing, flat, preferred_element_type=jnp.float32)


def gathered_plan(
    activations,
    key_value_weight,
    token_adapter_index,
    adapter_down_weight,
    adapter_up_weight,
    cotangent,
):
    adapter_holders = lax.axis_size("fsdp")
    tok_rows = activations.shape[0]
    slot_capacity = 2 * tok_rows // adapter_holders
    feature_width = activations.shape[1]
    output_width = cotangent.shape[1]
    placing = placement_matrix(token_adapter_index, adapter_holders, slot_capacity)
    down_resident = adapter_down_weight[0]
    up_resident = adapter_up_weight[0]
    whole_cot = lax.all_gather(cotangent, "tp", axis=1, tiled=True)
    whole_weight = lax.all_gather(key_value_weight, "fsdp", axis=0, tiled=True)
    partial_value = jnp.dot(activations, whole_weight.T, preferred_element_type=jnp.float32)
    base_gradient = jnp.dot(whole_cot, whole_weight, preferred_element_type=jnp.float32)
    base_output = lax.psum_scatter(
        partial_value.astype(jnp.bfloat16), "tp", scatter_dimension=1, tiled=True
    ).astype(jnp.float32)
    rows_send = pack_rows(placing, activations, adapter_holders)
    cot_send = pack_rows(placing, cotangent, adapter_holders)
    rows_recv = lax.all_to_all(rows_send, "fsdp", split_axis=0, concat_axis=0, tiled=True)
    rows_flat = rows_recv.reshape(-1, feature_width)
    low_part = jnp.dot(rows_flat, down_resident.T, preferred_element_type=jnp.float32)
    rank_activation = lax.psum(low_part.astype(jnp.bfloat16), "tp")
    adapter_output = (
        adapter_scale * jnp.dot(rank_activation, up_resident, preferred_element_type=jnp.float32)
    ).astype(jnp.bfloat16)
    out_back = lax.all_to_all(
        adapter_output.reshape(adapter_holders, slot_capacity, output_width),
        "fsdp",
        split_axis=0,
        concat_axis=0,
        tiled=True,
    )
    cot_recv = lax.all_to_all(cot_send, "fsdp", split_axis=0, concat_axis=0, tiled=True)
    flat_output_gradient = cot_recv.reshape(-1, output_width)
    backward_piece = adapter_scale * jnp.dot(
        flat_output_gradient, up_resident.T, preferred_element_type=jnp.float32
    )
    backward_result = lax.psum(backward_piece.astype(jnp.bfloat16), "tp")
    adapter_input = jnp.dot(
        backward_result, down_resident, preferred_element_type=jnp.float32
    ).astype(jnp.bfloat16)
    in_back = lax.all_to_all(
        adapter_input.reshape(adapter_holders, slot_capacity, feature_width),
        "fsdp",
        split_axis=0,
        concat_axis=0,
        tiled=True,
    )
    grad_down = jnp.einsum(
        "sr,sd->rd", backward_result, rows_flat, preferred_element_type=jnp.float32
    )
    up_gradient = adapter_scale * jnp.einsum(
        "sr,sk->rk", rank_activation, flat_output_gradient, preferred_element_type=jnp.float32
    )
    key_value_output = (base_output + unpack_rows(placing, out_back)).astype(jnp.bfloat16)
    input_gradient = (base_gradient + unpack_rows(placing, in_back)).astype(jnp.bfloat16)
    return (key_value_output, input_gradient, grad_down[None], up_gradient[None])


def nn(a, b):
    return lax.dot_general(a, b, (((1,), (0,)), ((), ())), preferred_element_type=f32)


def nt(a, b):
    return lax.dot_general(a, b, (((1,), (1,)), ((), ())), preferred_element_type=f32)


def tn(a, b):
    return lax.dot_general(a, b, (((0,), (0,)), ((), ())), preferred_element_type=f32)


def rows2(a, b):
    return jnp.concatenate([a, b], axis=0)


def swap(x, axis, bit):
    return lax.ppermute(x, axis, [(i, i ^ bit) for i in range(lax.axis_size(axis))])


def both(x, pairs):
    flat = [(4 * a[0] + 2 * a[1] + a[2], 4 * b[0] + 2 * b[1] + b[2]) for a, b in pairs]
    return lax.ppermute(x, ("fsdp", "tp"), flat)


def after(values, *earlier):
    return lax.optimization_barrier((values, earlier))[0]


Y, Z, IN_PAIR, ON_OWN = range(4)


def cost(us):
    return pl.CostEstimate(flops=us * 1_000_000_000, bytes_accessed=1000 + us * 3_000_000, transcendentals=0)


def local_kernel(body, outs, where, *args, us=0):
    single = not isinstance(outs, list)
    shapes = [jax.ShapeDtypeStruct(s, d) for s, d in ([outs] if single else outs)]
    got = pl.pallas_call(
        body,
        out_shape=shapes,
        in_specs=[pl.BlockSpec(memory_space=pltpu.SMEM)]
        + [pl.BlockSpec(memory_space=pltpu.VMEM)] * len(args),
        out_specs=[pl.BlockSpec(memory_space=pltpu.VMEM)] * len(shapes),
        compiler_params=pltpu.CompilerParams(vmem_limit_bytes=12 * 1024 * 1024),
        cost_estimate=cost(us),
    )(where, *args)
    return got[0] if single else got


def column_half(where, wide, arrays, counts, blocks):
    def body(where, *refs):
        place = 0
        for ref in refs[:-1]:
            refs[-1][place : place + ref.shape[0], :] = ref[...]
            place += ref.shape[0]

    def spec(count, block):
        return pl.BlockSpec((count, wide), lambda j, s: (block, s[Y]))

    total = sum(counts)
    return pl.pallas_call(
        body,
        grid_spec=pltpu.PrefetchScalarGridSpec(
            num_scalar_prefetch=1,
            grid=(1,),
            in_specs=[spec(n, b) for n, b in zip(counts, blocks)],
            out_specs=pl.BlockSpec((total, wide), lambda j, s: (0, 0)),
        ),
        out_shape=jax.ShapeDtypeStruct((total, wide), bf16),
        compiler_params=pltpu.CompilerParams(vmem_limit_bytes=12 * 1024 * 1024),
        cost_estimate=cost(0),
    )(where, *arrays)


def member(where, idx, rank):
    lane = lax.broadcasted_iota(jnp.int32, (idx.shape[0], 2 * rank), 1)
    z = where[Z]
    return idx == jnp.where(lane < rank, z, z ^ 1)


def column(row):
    n = row.shape[1]
    same = lax.broadcasted_iota(jnp.int32, (n, n), 0) == lax.broadcasted_iota(jnp.int32, (n, n), 1)
    picked = jnp.where(same, jnp.broadcast_to(row, (n, n)).astype(f32), 0.0)
    return jnp.sum(picked, axis=1, keepdims=True).astype(jnp.int32)


def back_kernel(where, cot, cot_got, idx, up, up_sib, out, members):
    width = cot.shape[1]
    toks = cot.shape[0]
    cot2 = rows2(cot[...], cot_got[:toks, :])
    part = adapter_scale * nt(cot2, rows2(up[...], up_sib[...]))
    idx_got = cot_got[toks:, :toks].astype(f32)[:1].astype(jnp.int32)
    mine = member(where, rows2(column(idx[...]), column(idx_got)), up.shape[0])
    members[...] = mine.astype(bf16)
    out[:, :width] = cot2
    out[:, width:] = jnp.where(mine, part, 0.0).astype(bf16)


def block_kernel(where, mine, got, out):
    width = out.shape[1] - 128
    in_pair = jnp.full((1, 1), where[IN_PAIR], jnp.int32) == 1
    out[:, :width] = jnp.where(in_pair, mine[:, :width], got[:, :width])
    out[:, width:] = (mine[:, width:].astype(f32) + got[:, width:].astype(f32)).astype(bf16)


def pair_blocks(where, mine, got):
    width = mine.shape[1] - 128
    on_own = jnp.full((1, 1), where[ON_OWN], jnp.int32) == 1
    a, b = mine[:, :width], got[:, :width]
    return jnp.where(on_own, a, b), jnp.where(on_own, b, a)


def whole_back(mine, got):
    width = mine.shape[1] - 128
    return (mine[:, width:].astype(f32) + got[:, width:].astype(f32)).astype(bf16)


def gradient_kernel(where, mine, got, weight, down, first, second, top, bottom):
    rank = down.shape[0]
    head = first.shape[0] - rank
    c_own, c_sib = pair_blocks(where, mine, got)
    back = whole_back(mine, got)
    g = nn(c_own, weight[...])
    g += nn(c_sib[:, :head], first[rank:, :])
    g += nn(c_sib[:, head:], second[...])
    g += nn(back, rows2(down[...], first[:rank, :]))
    toks = top.shape[0]
    top[...] = g[:toks].astype(bf16)
    bottom[...] = g[toks:].astype(bf16)


def gradient_half(where, side, mine, got, weight, down, first, second):
    toks, tile = mine.shape[0] // 2, 512
    steps = first.shape[1] // tile
    whole = lambda a: pl.BlockSpec(a.shape, lambda j, s: (0, 0))
    by_side = lambda a: pl.BlockSpec((a.shape[0], tile), lambda j, s: (0, s[4] * steps + j))
    tiled = lambda n: pl.BlockSpec((n, tile), lambda j, s: (0, j))
    return pl.pallas_call(
        gradient_kernel,
        grid_spec=pltpu.PrefetchScalarGridSpec(
            num_scalar_prefetch=1,
            grid=(steps,),
            in_specs=[
                whole(mine),
                whole(got),
                by_side(weight),
                by_side(down),
                tiled(first.shape[0]),
                tiled(second.shape[0]),
            ],
            out_specs=[tiled(toks), tiled(toks)],
        ),
        out_shape=[
            jax.ShapeDtypeStruct((toks, steps * tile), bf16),
            jax.ShapeDtypeStruct((toks, steps * tile), bf16),
        ],
        compiler_params=pltpu.CompilerParams(vmem_limit_bytes=12 * 1024 * 1024),
        cost_estimate=cost(0),
    )(jnp.concatenate([where, side[None]]), mine, got, weight, down, first, second)


def gradient_end_kernel(where, near, near_got, far, far_got, out):
    half = near.shape[1]
    y = where[Y]
    at = pl.ds(pl.multiple_of(y * half, half), half)
    out[:, at] = (near[...].astype(f32) + near_got[...].astype(f32)).astype(bf16)
    at = pl.ds(pl.multiple_of((1 - y) * half, half), half)
    out[:, at] = (far[...].astype(f32) + far_got[...].astype(f32)).astype(bf16)


def low_kernel(where, act, act_got, members, down, near, far, out):
    rank, half = down.shape[0], near.shape[1]
    y = where[Y]
    at_near = pl.ds(pl.multiple_of(y * half, half), half)
    at_far = pl.ds(pl.multiple_of((1 - y) * half, half), half)
    part = nt(rows2(act[:, at_near], act_got[:, at_near]), rows2(down[:, at_near], near[:rank, :]))
    part += nt(rows2(act[:, at_far], act_got[:, at_far]), rows2(down[:, at_far], far[:rank, :]))
    out[...] = jnp.where(members[...] != 0, part, 0.0).astype(bf16)


def adapter_kernel(
    where, give, give_got, mine, got, act, act_got, cot, cot_got, up, up_sib,
    lora, lora_far, down_own, up_own, sib, sib_end,
):
    rank, width, toks = up.shape[0], act.shape[1], act.shape[0]
    whole_low = whole_back(give, give_got)
    out = (adapter_scale * nn(whole_low, rows2(up[...], up_sib[...]))).astype(bf16)
    lora[...] = out[:toks]
    lora_far[...] = out[toks:]
    grad = tn(whole_back(mine, got), rows2(act[...], act_got[...]))
    down_own[...] = grad[:rank]
    cut = sib.shape[1]
    sib[...] = grad[rank:, :cut].astype(bf16)
    sib_end[:, : width - cut] = grad[rank:, cut:].astype(bf16)
    grad = adapter_scale * tn(whole_low, rows2(cot[...], cot_got[: cot.shape[0], :]))
    up_own[...] = grad[:rank]
    sib_end[:, width - cut :] = grad[rank:].astype(bf16)


def adapter_end_kernel(where, down_own, up_own, got, got_end, down_out, up_out):
    cut, rest = got.shape[1], down_own.shape[1] - got.shape[1]
    down_out[0, :, :cut] = down_own[:, :cut] + got[...].astype(f32)
    down_out[0, :, cut:] = down_own[:, cut:] + got_end[:, :rest].astype(f32)
    up_out[0] = up_own[...] + got_end[:, rest:].astype(f32)


def base_near_kernel(where, act, act_got, weight, first, second, out):
    rows = weight.shape[0]
    head = rows - second.shape[0]
    cut = first.shape[0] - head
    wide = first.shape[1]
    at = pl.ds(pl.multiple_of(where[Y] * wide, wide), wide)
    near = rows2(act[:, at], act_got[:, at])
    out[:, :rows] = nt(rows2(act[...], act_got[...]), weight[...])
    out[:, rows : rows + head] = nt(near, first[cut:, :])
    out[:, rows + head :] = nt(near, second[...])


def base_far_kernel(where, part, act, act_got, first, second, low, low_got, keep, give):
    rows = keep.shape[1]
    head = rows - second.shape[0]
    cut = first.shape[0] - head
    wide = first.shape[1]
    at = pl.ds(pl.multiple_of((1 - where[Y]) * wide, wide), wide)
    far = rows2(act[:, at], act_got[:, at])
    on_own = jnp.full((1, 1), where[ON_OWN], jnp.int32) == 1
    for lo, hi, block in ((0, head, first[cut:, :]), (head, rows, second[...])):
        mine = part[:, lo:hi]
        other = part[:, rows + lo : rows + hi] + nt(far, block)
        keep[:, lo:hi] = jnp.where(on_own, mine, other)
        give[:, lo:hi] = jnp.where(on_own, other, mine).astype(bf16)
    give[:, rows:] = (low[...].astype(f32) + low_got[...].astype(f32)).astype(bf16)


def held_kernel(where, keep, got, held):
    held[...] = (keep[...] + got[:, : keep.shape[1]].astype(f32)).astype(bf16)


def turn_kernel(where, held, got, lora_far, turn):
    toks = turn.shape[0]
    in_pair = jnp.full((1, 1), where[IN_PAIR], jnp.int32) == 1
    base = held[toks:, :].astype(f32) + got[toks:, :].astype(f32)
    turn[...] = (lora_far[...].astype(f32) + jnp.where(in_pair, base, 0.0)).astype(bf16)


def output_kernel(where, held, got, lora, turned, out):
    toks = out.shape[0]
    in_pair = jnp.full((1, 1), where[IN_PAIR], jnp.int32) == 1
    base = held[:toks, :].astype(f32) + got[:toks, :].astype(f32)
    total = turned[...].astype(f32) + jnp.where(in_pair, base, 0.0)
    out[...] = (total + lora[...].astype(f32)).astype(bf16)


def pair_plan(
    activations,
    key_value_weight,
    token_adapter_index,
    adapter_down_weight,
    adapter_up_weight,
    cotangent,
):
    z = lax.axis_index("fsdp")
    y = lax.axis_index("groups")
    t = lax.axis_index("tp")
    x, c = t // 2, t % 2
    where = jnp.stack([y, z, x == z // 2, c == z % 2]).astype(jnp.int32)
    rows, width = key_value_weight.shape
    toks, out_width = cotangent.shape
    half, wide = rows // 2, width // 2
    down = adapter_down_weight[0]
    up = adapter_up_weight[0]
    rank = down.shape[0]
    places = [(zz, xx, cc) for zz in range(4) for xx in range(2) for cc in range(2)]

    idx = token_adapter_index.reshape(1, toks)
    idx_row = jnp.pad(idx.astype(bf16), ((0, 15), (0, out_width - toks)))
    cot_got = swap(jnp.concatenate([cotangent, idx_row], axis=0), "fsdp", 2)
    up_sib = swap(up, "fsdp", 1)
    head = rows * 2 // 4
    piece0 = column_half(where, wide, (down, key_value_weight), (rank, head), (0, 0))
    piece1 = column_half(where, wide, (key_value_weight,), (rows - head,), (1,))
    near0 = swap(piece0, "fsdp", 1)
    act_got = swap(after(activations, cot_got, up_sib), "fsdp", 2)
    near1 = swap(after(piece1, cot_got, up_sib), "fsdp", 1)

    mine, members = local_kernel(
        back_kernel,
        [((2 * toks, out_width + 2 * rank), bf16), ((2 * toks, 2 * rank), bf16)],
        where,
        cotangent, cot_got, idx, up, up_sib, us=0,
    )
    mine_x = swap(mine, "tp", 2)
    near0 = after(near0, mine)
    far0 = swap(near0, "groups", 1)
    far1 = swap(near1, "groups", 1)
    mine_x = after(mine_x, near1)
    mine = local_kernel(block_kernel, (mine.shape, bf16), where, mine, mine_x)
    got = swap(mine, "tp", 1)

    near, near_sent = gradient_half(where, y, mine, got, key_value_weight, down, near0, near1)
    near_got = swap(near_sent, "fsdp", 2)

    act_got = after(act_got, near_sent)
    part = local_kernel(
        base_near_kernel, ((2 * toks, 2 * rows), f32), where,
        activations, act_got, key_value_weight, near0, near1, us=0,
    )

    far0 = after(far0, part)
    low = local_kernel(
        low_kernel, ((2 * toks, 2 * rank), bf16), where,
        activations, act_got, members, down, near0, far0,
    )
    low_x = swap(low, "tp", 2)

    far1 = after(far1, low)
    far, far_sent = gradient_half(where, 1 - y, mine, got, key_value_weight, down, far0, far1)
    far_got = swap(far_sent, "fsdp", 2)

    part, near_got = after((part, near_got), far_sent)
    keep, give = local_kernel(
        base_far_kernel,
        [((2 * toks, rows), f32), ((2 * toks, rows + 2 * rank), bf16)],
        where,
        part, activations, act_got, far0, far1, low, low_x, us=0,
    )
    give_got = swap(give, "tp", 1)
    held = local_kernel(held_kernel, ((2 * toks, rows), bf16), where, keep, give_got)
    held_got = both(held, [((a, b, d), (a, 1 - b, d)) for a, b, d in places if b != a // 2])

    give_got = after(give_got, held)
    lora, lora_far, down_own, up_own, sib, sib_end = local_kernel(
        adapter_kernel,
        [
            ((toks, out_width), bf16),
            ((toks, out_width), bf16),
            ((rank, width), f32),
            ((rank, out_width), f32),
            ((rank, (width + out_width) // 2), bf16),
            ((rank, (width + out_width) // 2), bf16),
        ],
        where,
        give, give_got, mine, got, activations, act_got, cotangent, cot_got, up, up_sib, us=0,
    )
    turn = local_kernel(
        turn_kernel, ((toks, out_width), bf16), where, held, held_got, lora_far
    )
    turned = swap(turn, "fsdp", 2)
    grad_down, up_gradient = local_kernel(
        adapter_end_kernel, [((1, rank, width), f32), ((1, rank, out_width), f32)], where,
        down_own, up_own, swap(sib, "fsdp", 1), swap(sib_end, "fsdp", 1),
    )

    input_gradient = local_kernel(
        gradient_end_kernel, ((toks, width), bf16), where, near, near_got, far, far_got
    )
    key_value_output = local_kernel(
        output_kernel, ((toks, out_width), bf16), where, held, held_got, lora, turned
    )
    return (key_value_output, input_gradient, grad_down, up_gradient)


def solution(mesh):
    paired = mesh.shape["fsdp"] == 4 and mesh.shape["tp"] == 4 and mesh.shape["groups"] == 2
    return jax.shard_map(
        pair_plan if paired else gathered_plan,
        mesh=mesh,
        in_specs=(
            P(("groups", "fsdp"), "tp"),
            P("fsdp", "tp"),
            P(("groups", "fsdp"), None),
            P("fsdp", None, "tp"),
            P("fsdp", None, "tp"),
            P(("groups", "fsdp"), "tp"),
        ),
        out_specs=(
            P(("groups", "fsdp"), "tp"),
            P(("groups", "fsdp"), "tp"),
            P(("groups", "fsdp"), None, "tp"),
            P(("groups", "fsdp"), None, "tp"),
        ),
        check_vma=False,
    )
```

```python
import jax
import jax.numpy as jnp
from jax import lax
from jax.experimental import pallas as pl
from jax.experimental.pallas import tpu as pltpu
from jax.sharding import PartitionSpec as P

adapter_scale = 2.0
f32 = jnp.float32
bf16 = jnp.bfloat16


def placement_matrix(token_adapter_index, adapter_holders, slot_capacity):
    owner_of = token_adapter_index[:, 0]
    shard_member = (
        owner_of[:, None] == jnp.arange(adapter_holders, dtype=jnp.int32)[None, :]
    ).astype(jnp.int32)
    earlier = jnp.cumsum(shard_member, axis=0) - shard_member
    within = jnp.sum(earlier * shard_member, axis=1)
    target = owner_of * slot_capacity + within
    return (
        jnp.arange(adapter_holders * slot_capacity, dtype=jnp.int32)[:, None] == target[None, :]
    ).astype(jnp.bfloat16)


def pack_rows(placing, values, adapter_holders):
    packed = jnp.dot(placing, values, preferred_element_type=jnp.float32).astype(jnp.bfloat16)
    return packed.reshape(adapter_holders, -1, values.shape[1])


def unpack_rows(placing, returned):
    flat = returned.reshape(-1, returned.shape[2])
    return jnp.einsum("st,sk->tk", placing, flat, preferred_element_type=jnp.float32)


def gathered_plan(
    activations,
    key_value_weight,
    token_adapter_index,
    adapter_down_weight,
    adapter_up_weight,
    cotangent,
):
    adapter_holders = lax.axis_size("fsdp")
    tok_rows = activations.shape[0]
    slot_capacity = 2 * tok_rows // adapter_holders
    feature_width = activations.shape[1]
    output_width = cotangent.shape[1]
    placing = placement_matrix(token_adapter_index, adapter_holders, slot_capacity)
    down_resident = adapter_down_weight[0]
    up_resident = adapter_up_weight[0]
    whole_cot = lax.all_gather(cotangent, "tp", axis=1, tiled=True)
    whole_weight = lax.all_gather(key_value_weight, "fsdp", axis=0, tiled=True)
    partial_value = jnp.dot(activations, whole_weight.T, preferred_element_type=jnp.float32)
    base_gradient = jnp.dot(whole_cot, whole_weight, preferred_element_type=jnp.float32)
    base_output = lax.psum_scatter(
        partial_value.astype(jnp.bfloat16), "tp", scatter_dimension=1, tiled=True
    ).astype(jnp.float32)
    rows_send = pack_rows(placing, activations, adapter_holders)
    cot_send = pack_rows(placing, cotangent, adapter_holders)
    rows_recv = lax.all_to_all(rows_send, "fsdp", split_axis=0, concat_axis=0, tiled=True)
    rows_flat = rows_recv.reshape(-1, feature_width)
    low_part = jnp.dot(rows_flat, down_resident.T, preferred_element_type=jnp.float32)
    rank_activation = lax.psum(low_part.astype(jnp.bfloat16), "tp")
    adapter_output = (
        adapter_scale * jnp.dot(rank_activation, up_resident, preferred_element_type=jnp.float32)
    ).astype(jnp.bfloat16)
    out_back = lax.all_to_all(
        adapter_output.reshape(adapter_holders, slot_capacity, output_width),
        "fsdp",
        split_axis=0,
        concat_axis=0,
        tiled=True,
    )
    cot_recv = lax.all_to_all(cot_send, "fsdp", split_axis=0, concat_axis=0, tiled=True)
    flat_output_gradient = cot_recv.reshape(-1, output_width)
    backward_piece = adapter_scale * jnp.dot(
        flat_output_gradient, up_resident.T, preferred_element_type=jnp.float32
    )
    backward_result = lax.psum(backward_piece.astype(jnp.bfloat16), "tp")
    adapter_input = jnp.dot(
        backward_result, down_resident, preferred_element_type=jnp.float32
    ).astype(jnp.bfloat16)
    in_back = lax.all_to_all(
        adapter_input.reshape(adapter_holders, slot_capacity, feature_width),
        "fsdp",
        split_axis=0,
        concat_axis=0,
        tiled=True,
    )
    grad_down = jnp.einsum(
        "sr,sd->rd", backward_result, rows_flat, preferred_element_type=jnp.float32
    )
    up_gradient = adapter_scale * jnp.einsum(
        "sr,sk->rk", rank_activation, flat_output_gradient, preferred_element_type=jnp.float32
    )
    key_value_output = (base_output + unpack_rows(placing, out_back)).astype(jnp.bfloat16)
    input_gradient = (base_gradient + unpack_rows(placing, in_back)).astype(jnp.bfloat16)
    return (key_value_output, input_gradient, grad_down[None], up_gradient[None])


def nn(a, b):
    return lax.dot_general(a, b, (((1,), (0,)), ((), ())), preferred_element_type=f32)


def nt(a, b):
    return lax.dot_general(a, b, (((1,), (1,)), ((), ())), preferred_element_type=f32)


def tn(a, b):
    return lax.dot_general(a, b, (((0,), (0,)), ((), ())), preferred_element_type=f32)


def rows2(a, b):
    return jnp.concatenate([a, b], axis=0)


def swap(x, axis, bit):
    return lax.ppermute(x, axis, [(i, i ^ bit) for i in range(lax.axis_size(axis))])


def both(x, pairs):
    flat = [(4 * a[0] + 2 * a[1] + a[2], 4 * b[0] + 2 * b[1] + b[2]) for a, b in pairs]
    return lax.ppermute(x, ("fsdp", "tp"), flat)


def after(values, *earlier):
    return lax.optimization_barrier((values, earlier))[0]


Y, Z, IN_PAIR, ON_OWN = range(4)


def cost(us):
    return pl.CostEstimate(flops=us * 1_000_000_000, bytes_accessed=1000 + us * 3_000_000, transcendentals=0)


def local_kernel(body, outs, where, *args, us=0):
    single = not isinstance(outs, list)
    shapes = [jax.ShapeDtypeStruct(s, d) for s, d in ([outs] if single else outs)]
    got = pl.pallas_call(
        body,
        out_shape=shapes,
        in_specs=[pl.BlockSpec(memory_space=pltpu.SMEM)]
        + [pl.BlockSpec(memory_space=pltpu.VMEM)] * len(args),
        out_specs=[pl.BlockSpec(memory_space=pltpu.VMEM)] * len(shapes),
        compiler_params=pltpu.CompilerParams(vmem_limit_bytes=12 * 1024 * 1024),
        cost_estimate=cost(us),
    )(where, *args)
    return got[0] if single else got


def column_half(where, wide, arrays, counts, blocks):
    def body(where, *refs):
        place = 0
        for ref in refs[:-1]:
            refs[-1][place : place + ref.shape[0], :] = ref[...]
            place += ref.shape[0]

    def spec(count, block):
        return pl.BlockSpec((count, wide), lambda j, s: (block, s[Y]))

    total = sum(counts)
    return pl.pallas_call(
        body,
        grid_spec=pltpu.PrefetchScalarGridSpec(
            num_scalar_prefetch=1,
            grid=(1,),
            in_specs=[spec(n, b) for n, b in zip(counts, blocks)],
            out_specs=pl.BlockSpec((total, wide), lambda j, s: (0, 0)),
        ),
        out_shape=jax.ShapeDtypeStruct((total, wide), bf16),
        compiler_params=pltpu.CompilerParams(vmem_limit_bytes=12 * 1024 * 1024),
        cost_estimate=cost(0),
    )(where, *arrays)


def member(where, idx, rank):
    lane = lax.broadcasted_iota(jnp.int32, (idx.shape[0], 2 * rank), 1)
    z = where[Z]
    return idx == jnp.where(lane < rank, z, z ^ 1)


def column(row):
    n = row.shape[1]
    same = lax.broadcasted_iota(jnp.int32, (n, n), 0) == lax.broadcasted_iota(jnp.int32, (n, n), 1)
    picked = jnp.where(same, jnp.broadcast_to(row, (n, n)).astype(f32), 0.0)
    return jnp.sum(picked, axis=1, keepdims=True).astype(jnp.int32)


def back_kernel(where, cot, cot_got, idx, up, up_sib, out, members):
    width = cot.shape[1]
    toks = cot.shape[0]
    cot2 = rows2(cot[...], cot_got[:toks, :])
    part = adapter_scale * nt(cot2, rows2(up[...], up_sib[...]))
    idx_got = cot_got[toks:, :toks].astype(f32)[:1].astype(jnp.int32)
    mine = member(where, rows2(column(idx[...]), column(idx_got)), up.shape[0])
    members[...] = mine.astype(bf16)
    out[:, :width] = cot2
    out[:, width:] = jnp.where(mine, part, 0.0).astype(bf16)


def block_kernel(where, mine, got, out):
    width = out.shape[1] - 128
    in_pair = jnp.full((1, 1), where[IN_PAIR], jnp.int32) == 1
    out[:, :width] = jnp.where(in_pair, mine[:, :width], got[:, :width])
    out[:, width:] = (mine[:, width:].astype(f32) + got[:, width:].astype(f32)).astype(bf16)


def pair_blocks(where, mine, got):
    width = mine.shape[1] - 128
    on_own = jnp.full((1, 1), where[ON_OWN], jnp.int32) == 1
    a, b = mine[:, :width], got[:, :width]
    return jnp.where(on_own, a, b), jnp.where(on_own, b, a)


def whole_back(mine, got):
    width = mine.shape[1] - 128
    return (mine[:, width:].astype(f32) + got[:, width:].astype(f32)).astype(bf16)


def gradient_kernel(where, mine, got, weight, down, first, second, top, bottom):
    rank = down.shape[0]
    head = first.shape[0] - rank
    c_own, c_sib = pair_blocks(where, mine, got)
    back = whole_back(mine, got)
    g = nn(c_own, weight[...])
    g += nn(c_sib[:, :head], first[rank:, :])
    g += nn(c_sib[:, head:], second[...])
    g += nn(back, rows2(down[...], first[:rank, :]))
    toks = top.shape[0]
    top[...] = g[:toks].astype(bf16)
    bottom[...] = g[toks:].astype(bf16)


def gradient_half(where, side, mine, got, weight, down, first, second):
    toks, tile = mine.shape[0] // 2, 512
    steps = first.shape[1] // tile
    whole = lambda a: pl.BlockSpec(a.shape, lambda j, s: (0, 0))
    by_side = lambda a: pl.BlockSpec((a.shape[0], tile), lambda j, s: (0, s[4] * steps + j))
    tiled = lambda n: pl.BlockSpec((n, tile), lambda j, s: (0, j))
    return pl.pallas_call(
        gradient_kernel,
        grid_spec=pltpu.PrefetchScalarGridSpec(
            num_scalar_prefetch=1,
            grid=(steps,),
            in_specs=[
                whole(mine),
                whole(got),
                by_side(weight),
                by_side(down),
                tiled(first.shape[0]),
                tiled(second.shape[0]),
            ],
            out_specs=[tiled(toks), tiled(toks)],
        ),
        out_shape=[
            jax.ShapeDtypeStruct((toks, steps * tile), bf16),
            jax.ShapeDtypeStruct((toks, steps * tile), bf16),
        ],
        compiler_params=pltpu.CompilerParams(vmem_limit_bytes=56 * 1024 * 1024),
        cost_estimate=cost(0),
    )(jnp.concatenate([where, side[None]]), mine, got, weight, down, first, second)


def gradient_end_kernel(where, near, near_got, far, far_got, out):
    half = near.shape[1]
    y = where[Y]
    at = pl.ds(pl.multiple_of(y * half, half), half)
    out[:, at] = (near[...].astype(f32) + near_got[...].astype(f32)).astype(bf16)
    at = pl.ds(pl.multiple_of((1 - y) * half, half), half)
    out[:, at] = (far[...].astype(f32) + far_got[...].astype(f32)).astype(bf16)


def low_kernel(where, act, act_got, members, down, near, far, out):
    rank, half = down.shape[0], near.shape[1]
    y = where[Y]
    at_near = pl.ds(pl.multiple_of(y * half, half), half)
    at_far = pl.ds(pl.multiple_of((1 - y) * half, half), half)
    part = nt(rows2(act[:, at_near], act_got[:, at_near]), rows2(down[:, at_near], near[:rank, :]))
    part += nt(rows2(act[:, at_far], act_got[:, at_far]), rows2(down[:, at_far], far[:rank, :]))
    out[...] = jnp.where(members[...] != 0, part, 0.0).astype(bf16)


def low_part(where, act, act_got, members, down, near, far):
    whole = lambda a: pl.BlockSpec(a.shape, lambda j: (0, 0))
    head = pl.BlockSpec((down.shape[0], near.shape[1]), lambda j: (0, 0))
    return pl.pallas_call(
        low_kernel,
        grid=(1,),
        in_specs=[pl.BlockSpec(memory_space=pltpu.SMEM)]
        + [whole(a) for a in (act, act_got, members, down)]
        + [head, head],
        out_specs=whole(members),
        out_shape=jax.ShapeDtypeStruct(members.shape, bf16),
        compiler_params=pltpu.CompilerParams(vmem_limit_bytes=12 * 1024 * 1024),
        cost_estimate=cost(0),
    )(where, act, act_got, members, down, near, far)


def adapter_kernel(
    where, give, give2, give_got, give_got2, mine, got, act, act_got, cot, cot_got, up, up_sib,
    lora, lora_far, down_own, up_own, sib, sib_end,
):
    rank, width, toks = up.shape[0], act.shape[1], act.shape[0]
    whole_low = rows2(whole_back(give, give_got), whole_back(give2, give_got2))
    out = (adapter_scale * nn(whole_low, rows2(up[...], up_sib[...]))).astype(bf16)
    lora[...] = out[:toks]
    lora_far[...] = out[toks:]
    grad = tn(whole_back(mine, got), rows2(act[...], act_got[...]))
    down_own[...] = grad[:rank]
    cut = sib.shape[1]
    sib[...] = grad[rank:, :cut].astype(bf16)
    sib_end[:, : width - cut] = grad[rank:, cut:].astype(bf16)
    grad = adapter_scale * tn(whole_low, rows2(cot[...], cot_got[: cot.shape[0], :]))
    up_own[...] = grad[:rank]
    sib_end[:, width - cut :] = grad[rank:].astype(bf16)


def adapter_end_kernel(where, down_own, up_own, got, got_end, down_out, up_out):
    cut, rest = got.shape[1], down_own.shape[1] - got.shape[1]
    down_out[0, :, :cut] = down_own[:, :cut] + got[...].astype(f32)
    down_out[0, :, cut:] = down_own[:, cut:] + got_end[:, :rest].astype(f32)
    up_out[0] = up_own[...] + got_end[:, rest:].astype(f32)


def base_near_kernel(where, act, act_got, weight, first, second, out):
    rows = weight.shape[0]
    head = rows - second.shape[0]
    cut = first.shape[0] - head
    wide = first.shape[1]
    at = pl.ds(pl.multiple_of(where[Y] * wide, wide), wide)
    near = rows2(act[:, at], act_got[:, at])
    out[:, :rows] = nt(rows2(act[...], act_got[...]), weight[...])
    out[:, rows : rows + head] = nt(near, first[cut:, :])
    out[:, rows + head :] = nt(near, second[...])


def base_far_kernel(where, part, act, act_got, first, second, low, low_got, keep, give, give2):
    rows = keep.shape[1]
    head = rows - second.shape[0]
    cut = first.shape[0] - head
    wide = first.shape[1]
    at = pl.ds(pl.multiple_of((1 - where[Y]) * wide, wide), wide)
    far = rows2(act[:, at], act_got[:, at])
    on_own = jnp.full((1, 1), where[ON_OWN], jnp.int32) == 1
    for lo, hi, block in ((0, head, first[cut:, :]), (head, rows, second[...])):
        mine = part[:, lo:hi]
        other = part[:, rows + lo : rows + hi] + nt(far, block)
        keep[:, lo:hi] = jnp.where(on_own, mine, other)
        out = jnp.where(on_own, other, mine).astype(bf16)
        give[:, lo:hi] = out[: give.shape[0]]
        give2[:, lo:hi] = out[give.shape[0] :]
    total = (low[...].astype(f32) + low_got[...].astype(f32)).astype(bf16)
    give[:, rows:] = total[: give.shape[0]]
    give2[:, rows:] = total[give.shape[0] :]


def held_kernel(where, keep, got, got2, here, there):
    toks = here.shape[0]
    held = (keep[...] + rows2(got[...], got2[...])[:, : keep.shape[1]].astype(f32)).astype(bf16)
    here[...] = held[:toks]
    there[...] = held[toks:]


def turn_kernel(where, held, got, lora_far, turn):
    in_pair = jnp.full((1, 1), where[IN_PAIR], jnp.int32) == 1
    base = held[...].astype(f32) + got[...].astype(f32)
    turn[...] = (lora_far[...].astype(f32) + jnp.where(in_pair, base, 0.0)).astype(bf16)


def output_kernel(where, held, got, lora, turned, out):
    in_pair = jnp.full((1, 1), where[IN_PAIR], jnp.int32) == 1
    base = held[...].astype(f32) + got[...].astype(f32)
    total = turned[...].astype(f32) + jnp.where(in_pair, base, 0.0)
    out[...] = (total + lora[...].astype(f32)).astype(bf16)


def pair_plan(
    activations,
    key_value_weight,
    token_adapter_index,
    adapter_down_weight,
    adapter_up_weight,
    cotangent,
):
    z = lax.axis_index("fsdp")
    y = lax.axis_index("groups")
    t = lax.axis_index("tp")
    x, c = t // 2, t % 2
    where = jnp.stack([y, z, x == z // 2, c == z % 2]).astype(jnp.int32)
    rows, width = key_value_weight.shape
    toks, out_width = cotangent.shape
    half, wide = rows // 2, width // 2
    down = adapter_down_weight[0]
    up = adapter_up_weight[0]
    rank = down.shape[0]
    places = [(zz, xx, cc) for zz in range(4) for xx in range(2) for cc in range(2)]

    idx = token_adapter_index.reshape(1, toks)
    idx_row = jnp.pad(idx.astype(bf16), ((0, 15), (0, out_width - toks)))
    cot_got = swap(jnp.concatenate([cotangent, idx_row], axis=0), "fsdp", 2)
    up_sib = swap(up, "fsdp", 1)
    head = rows * 2 // 4
    piece0 = column_half(where, wide, (down, key_value_weight), (rank, head), (0, 0))
    piece1 = column_half(where, wide, (key_value_weight,), (rows - head,), (1,))
    near0 = swap(piece0, "fsdp", 1)
    act_got = swap(after(activations, cot_got, up_sib), "fsdp", 2)
    near1 = swap(after(piece1, cot_got, up_sib), "fsdp", 1)

    mine, members = local_kernel(
        back_kernel,
        [((2 * toks, out_width + 2 * rank), bf16), ((2 * toks, 2 * rank), bf16)],
        where,
        cotangent, cot_got, idx, up, up_sib, us=0,
    )
    mine_x = swap(mine, "tp", 2)
    near0 = after(near0, mine)
    far0 = swap(near0, "groups", 1)
    far1 = swap(near1, "groups", 1)
    mine_x = after(mine_x, near1)
    mine = local_kernel(block_kernel, (mine.shape, bf16), where, mine, mine_x)
    got = swap(mine, "tp", 1)

    near, near_sent = gradient_half(where, y, mine, got, key_value_weight, down, near0, near1)
    near_got = swap(near_sent, "fsdp", 2)

    act_got = after(act_got, near_sent)
    part = local_kernel(
        base_near_kernel, ((2 * toks, 2 * rows), f32), where,
        activations, act_got, key_value_weight, near0, near1, us=0,
    )

    far0 = after(far0, part)
    low = low_part(where, activations, act_got, members, down, near0, far0)
    low_x = swap(low, "tp", 2)

    far1 = after(far1, low)
    far, far_sent = gradient_half(where, 1 - y, mine, got, key_value_weight, down, far0, far1)
    far_got = swap(far_sent, "fsdp", 2)

    part = after(part, far_sent)
    keep, give, give2 = local_kernel(
        base_far_kernel,
        [((2 * toks, rows), f32)] + [((toks, rows + 2 * rank), bf16)] * 2,
        where,
        part, activations, act_got, far0, far1, low, low_x, us=0,
    )
    keep, near_got = after((keep, near_got), give)
    give_got, give_got2 = swap(give, "tp", 1), swap(give2, "tp", 1)
    here, there = local_kernel(held_kernel, [((toks, rows), bf16)] * 2, where, keep, give_got, give_got2)
    inward = [((a, b, d), (a, 1 - b, d)) for a, b, d in places if b != a // 2]
    there_got = both(there, inward)
    here_got = both(here, inward)
    held = here

    give_got = after(give_got, held)
    lora, lora_far, down_own, up_own, sib, sib_end = local_kernel(
        adapter_kernel,
        [
            ((toks, out_width), bf16),
            ((toks, out_width), bf16),
            ((rank, width), f32),
            ((rank, out_width), f32),
            ((rank, (width + out_width) // 2), bf16),
            ((rank, (width + out_width) // 2), bf16),
        ],
        where,
        give, give2, give_got, give_got2, mine, got, activations, act_got, cotangent, cot_got, up, up_sib, us=0,
    )
    turn = local_kernel(
        turn_kernel, ((toks, out_width), bf16), where, there, there_got, lora_far
    )
    turned = swap(turn, "fsdp", 2)
    grad_down, up_gradient = local_kernel(
        adapter_end_kernel, [((1, rank, width), f32), ((1, rank, out_width), f32)], where,
        down_own, up_own, swap(sib, "fsdp", 1), swap(sib_end, "fsdp", 1),
    )

    input_gradient = local_kernel(
        gradient_end_kernel, ((toks, width), bf16), where, near, near_got, far, far_got
    )
    key_value_output = local_kernel(
        output_kernel, ((toks, out_width), bf16), where, here, here_got, lora, turned
    )
    return (key_value_output, input_gradient, grad_down, up_gradient)


def solution(mesh):
    paired = mesh.shape["fsdp"] == 4 and mesh.shape["tp"] == 4 and mesh.shape["groups"] == 2
    return jax.shard_map(
        pair_plan if paired else gathered_plan,
        mesh=mesh,
        in_specs=(
            P(("groups", "fsdp"), "tp"),
            P("fsdp", "tp"),
            P(("groups", "fsdp"), None),
            P("fsdp", None, "tp"),
            P("fsdp", None, "tp"),
            P(("groups", "fsdp"), "tp"),
        ),
        out_specs=(
            P(("groups", "fsdp"), "tp"),
            P(("groups", "fsdp"), "tp"),
            P(("groups", "fsdp"), None, "tp"),
            P(("groups", "fsdp"), None, "tp"),
        ),
        check_vma=False,
    )
```

```python
import jax
import jax.numpy as jnp
from jax import lax
from jax.experimental import pallas as pl
from jax.experimental.pallas import tpu as pltpu
from jax.sharding import PartitionSpec as P

adapter_scale = 2.0
f32 = jnp.float32
bf16 = jnp.bfloat16


def placement_matrix(token_adapter_index, adapter_holders, slot_capacity):
    owner_of = token_adapter_index[:, 0]
    shard_member = (
        owner_of[:, None] == jnp.arange(adapter_holders, dtype=jnp.int32)[None, :]
    ).astype(jnp.int32)
    earlier = jnp.cumsum(shard_member, axis=0) - shard_member
    within = jnp.sum(earlier * shard_member, axis=1)
    target = owner_of * slot_capacity + within
    return (
        jnp.arange(adapter_holders * slot_capacity, dtype=jnp.int32)[:, None] == target[None, :]
    ).astype(jnp.bfloat16)


def pack_rows(placing, values, adapter_holders):
    packed = jnp.dot(placing, values, preferred_element_type=jnp.float32).astype(jnp.bfloat16)
    return packed.reshape(adapter_holders, -1, values.shape[1])


def unpack_rows(placing, returned):
    flat = returned.reshape(-1, returned.shape[2])
    return jnp.einsum("st,sk->tk", placing, flat, preferred_element_type=jnp.float32)


def gathered_plan(
    activations,
    key_value_weight,
    token_adapter_index,
    adapter_down_weight,
    adapter_up_weight,
    cotangent,
):
    adapter_holders = lax.axis_size("fsdp")
    tok_rows = activations.shape[0]
    slot_capacity = 2 * tok_rows // adapter_holders
    feature_width = activations.shape[1]
    output_width = cotangent.shape[1]
    placing = placement_matrix(token_adapter_index, adapter_holders, slot_capacity)
    down_resident = adapter_down_weight[0]
    up_resident = adapter_up_weight[0]
    whole_cot = lax.all_gather(cotangent, "tp", axis=1, tiled=True)
    whole_weight = lax.all_gather(key_value_weight, "fsdp", axis=0, tiled=True)
    partial_value = jnp.dot(activations, whole_weight.T, preferred_element_type=jnp.float32)
    base_gradient = jnp.dot(whole_cot, whole_weight, preferred_element_type=jnp.float32)
    base_output = lax.psum_scatter(
        partial_value.astype(jnp.bfloat16), "tp", scatter_dimension=1, tiled=True
    ).astype(jnp.float32)
    rows_send = pack_rows(placing, activations, adapter_holders)
    cot_send = pack_rows(placing, cotangent, adapter_holders)
    rows_recv = lax.all_to_all(rows_send, "fsdp", split_axis=0, concat_axis=0, tiled=True)
    rows_flat = rows_recv.reshape(-1, feature_width)
    low_part = jnp.dot(rows_flat, down_resident.T, preferred_element_type=jnp.float32)
    rank_activation = lax.psum(low_part.astype(jnp.bfloat16), "tp")
    adapter_output = (
        adapter_scale * jnp.dot(rank_activation, up_resident, preferred_element_type=jnp.float32)
    ).astype(jnp.bfloat16)
    out_back = lax.all_to_all(
        adapter_output.reshape(adapter_holders, slot_capacity, output_width),
        "fsdp",
        split_axis=0,
        concat_axis=0,
        tiled=True,
    )
    cot_recv = lax.all_to_all(cot_send, "fsdp", split_axis=0, concat_axis=0, tiled=True)
    flat_output_gradient = cot_recv.reshape(-1, output_width)
    backward_piece = adapter_scale * jnp.dot(
        flat_output_gradient, up_resident.T, preferred_element_type=jnp.float32
    )
    backward_result = lax.psum(backward_piece.astype(jnp.bfloat16), "tp")
    adapter_input = jnp.dot(
        backward_result, down_resident, preferred_element_type=jnp.float32
    ).astype(jnp.bfloat16)
    in_back = lax.all_to_all(
        adapter_input.reshape(adapter_holders, slot_capacity, feature_width),
        "fsdp",
        split_axis=0,
        concat_axis=0,
        tiled=True,
    )
    grad_down = jnp.einsum(
        "sr,sd->rd", backward_result, rows_flat, preferred_element_type=jnp.float32
    )
    up_gradient = adapter_scale * jnp.einsum(
        "sr,sk->rk", rank_activation, flat_output_gradient, preferred_element_type=jnp.float32
    )
    key_value_output = (base_output + unpack_rows(placing, out_back)).astype(jnp.bfloat16)
    input_gradient = (base_gradient + unpack_rows(placing, in_back)).astype(jnp.bfloat16)
    return (key_value_output, input_gradient, grad_down[None], up_gradient[None])


def nn(a, b):
    return lax.dot_general(a, b, (((1,), (0,)), ((), ())), preferred_element_type=f32)


def nt(a, b):
    return lax.dot_general(a, b, (((1,), (1,)), ((), ())), preferred_element_type=f32)


def tn(a, b):
    return lax.dot_general(a, b, (((0,), (0,)), ((), ())), preferred_element_type=f32)


def rows2(a, b):
    return jnp.concatenate([a, b], axis=0)


def swap(x, axis, bit):
    return lax.ppermute(x, axis, [(i, i ^ bit) for i in range(lax.axis_size(axis))])


def both(x, pairs):
    flat = [(4 * a[0] + 2 * a[1] + a[2], 4 * b[0] + 2 * b[1] + b[2]) for a, b in pairs]
    return lax.ppermute(x, ("fsdp", "tp"), flat)


def after(values, *earlier):
    return lax.optimization_barrier((values, earlier))[0]


Y, Z, IN_PAIR, ON_OWN = range(4)


SMALL = pl.CostEstimate(flops=0, bytes_accessed=1000, transcendentals=0)


def local_kernel(body, outs, where, *args):
    single = not isinstance(outs, list)
    shapes = [jax.ShapeDtypeStruct(s, d) for s, d in ([outs] if single else outs)]
    got = pl.pallas_call(
        body,
        out_shape=shapes,
        in_specs=[pl.BlockSpec(memory_space=pltpu.SMEM)]
        + [pl.BlockSpec(memory_space=pltpu.VMEM)] * len(args),
        out_specs=[pl.BlockSpec(memory_space=pltpu.VMEM)] * len(shapes),
        compiler_params=pltpu.CompilerParams(vmem_limit_bytes=12 * 1024 * 1024),
        cost_estimate=SMALL,
    )(where, *args)
    return got[0] if single else got


def column_half(where, wide, arrays, counts, blocks):
    def body(where, *refs):
        place = 0
        for ref in refs[:-1]:
            refs[-1][place : place + ref.shape[0], :] = ref[...]
            place += ref.shape[0]

    def spec(count, block):
        return pl.BlockSpec((count, wide), lambda j, s: (block, s[Y]))

    total = sum(counts)
    return pl.pallas_call(
        body,
        grid_spec=pltpu.PrefetchScalarGridSpec(
            num_scalar_prefetch=1,
            grid=(1,),
            in_specs=[spec(n, b) for n, b in zip(counts, blocks)],
            out_specs=pl.BlockSpec((total, wide), lambda j, s: (0, 0)),
        ),
        out_shape=jax.ShapeDtypeStruct((total, wide), bf16),
        compiler_params=pltpu.CompilerParams(vmem_limit_bytes=12 * 1024 * 1024),
        cost_estimate=SMALL,
    )(where, *arrays)


def member(where, idx, rank):
    lane = lax.broadcasted_iota(jnp.int32, (idx.shape[0], 2 * rank), 1)
    z = where[Z]
    return idx == jnp.where(lane < rank, z, z ^ 1)


def column(row):
    n = row.shape[1]
    same = lax.broadcasted_iota(jnp.int32, (n, n), 0) == lax.broadcasted_iota(jnp.int32, (n, n), 1)
    picked = jnp.where(same, jnp.broadcast_to(row, (n, n)).astype(f32), 0.0)
    return jnp.sum(picked, axis=1, keepdims=True).astype(jnp.int32)


def back_kernel(where, cot, cot_got, idx, up, up_sib, out, members):
    width = cot.shape[1]
    toks = cot.shape[0]
    cot2 = rows2(cot[...], cot_got[:toks, :])
    part = adapter_scale * nt(cot2, rows2(up[...], up_sib[...]))
    idx_got = cot_got[toks:, :toks].astype(f32)[:1].astype(jnp.int32)
    mine = member(where, rows2(column(idx[...]), column(idx_got)), up.shape[0])
    members[...] = mine.astype(bf16)
    out[:, :width] = cot2
    out[:, width:] = jnp.where(mine, part, 0.0).astype(bf16)


def block_kernel(where, mine, got, out):
    width = out.shape[1] - 128
    in_pair = jnp.full((1, 1), where[IN_PAIR], jnp.int32) == 1
    out[:, :width] = jnp.where(in_pair, mine[:, :width], got[:, :width])
    out[:, width:] = (mine[:, width:].astype(f32) + got[:, width:].astype(f32)).astype(bf16)


def pair_blocks(where, mine, got):
    width = mine.shape[1] - 128
    on_own = jnp.full((1, 1), where[ON_OWN], jnp.int32) == 1
    a, b = mine[:, :width], got[:, :width]
    return jnp.where(on_own, a, b), jnp.where(on_own, b, a)


def whole_back(mine, got):
    width = mine.shape[1] - 128
    return (mine[:, width:].astype(f32) + got[:, width:].astype(f32)).astype(bf16)


def gradient_kernel(where, mine, got, weight, down, first, second, top, bottom):
    rank = down.shape[0]
    head = first.shape[0] - rank
    c_own, c_sib = pair_blocks(where, mine, got)
    back = whole_back(mine, got)
    g = nn(c_own, weight[...])
    g += nn(c_sib[:, :head], first[rank:, :])
    g += nn(c_sib[:, head:], second[...])
    g += nn(back, rows2(down[...], first[:rank, :]))
    toks = top.shape[0]
    top[...] = g[:toks].astype(bf16)
    bottom[...] = g[toks:].astype(bf16)


def gradient_half(where, side, mine, got, weight, down, first, second):
    toks, tile = mine.shape[0] // 2, 512
    steps = first.shape[1] // tile
    whole = lambda a: pl.BlockSpec(a.shape, lambda j, s: (0, 0))
    by_side = lambda a: pl.BlockSpec((a.shape[0], tile), lambda j, s: (0, s[4] * steps + j))
    tiled = lambda n: pl.BlockSpec((n, tile), lambda j, s: (0, j))
    return pl.pallas_call(
        gradient_kernel,
        grid_spec=pltpu.PrefetchScalarGridSpec(
            num_scalar_prefetch=1,
            grid=(steps,),
            in_specs=[
                whole(mine),
                whole(got),
                by_side(weight),
                by_side(down),
                tiled(first.shape[0]),
                tiled(second.shape[0]),
            ],
            out_specs=[tiled(toks), tiled(toks)],
        ),
        out_shape=[
            jax.ShapeDtypeStruct((toks, steps * tile), bf16),
            jax.ShapeDtypeStruct((toks, steps * tile), bf16),
        ],
        compiler_params=pltpu.CompilerParams(vmem_limit_bytes=56 * 1024 * 1024),
        cost_estimate=SMALL,
    )(jnp.concatenate([where, side[None]]), mine, got, weight, down, first, second)


def gradient_end_kernel(where, near, near_got, far, far_got, out):
    half = near.shape[1]
    y = where[Y]
    at = pl.ds(pl.multiple_of(y * half, half), half)
    out[:, at] = (near[...].astype(f32) + near_got[...].astype(f32)).astype(bf16)
    at = pl.ds(pl.multiple_of((1 - y) * half, half), half)
    out[:, at] = (far[...].astype(f32) + far_got[...].astype(f32)).astype(bf16)


def low_kernel(where, act, act_got, members, down, near, far, out):
    rank, half = down.shape[0], near.shape[1]
    y = where[Y]
    at_near = pl.ds(pl.multiple_of(y * half, half), half)
    at_far = pl.ds(pl.multiple_of((1 - y) * half, half), half)
    part = nt(rows2(act[:, at_near], act_got[:, at_near]), rows2(down[:, at_near], near[:rank, :]))
    part += nt(rows2(act[:, at_far], act_got[:, at_far]), rows2(down[:, at_far], far[:rank, :]))
    out[...] = jnp.where(members[...] != 0, part, 0.0).astype(bf16)


def low_part(where, act, act_got, members, down, near, far):
    whole = lambda a: pl.BlockSpec(a.shape, lambda j: (0, 0))
    head = pl.BlockSpec((down.shape[0], near.shape[1]), lambda j: (0, 0))
    return pl.pallas_call(
        low_kernel,
        grid=(1,),
        in_specs=[pl.BlockSpec(memory_space=pltpu.SMEM)]
        + [whole(a) for a in (act, act_got, members, down)]
        + [head, head],
        out_specs=whole(members),
        out_shape=jax.ShapeDtypeStruct(members.shape, bf16),
        compiler_params=pltpu.CompilerParams(vmem_limit_bytes=12 * 1024 * 1024),
        cost_estimate=SMALL,
    )(where, act, act_got, members, down, near, far)


def adapter_kernel(
    where, give, give2, give_got, give_got2, mine, got, act, act_got, cot, cot_got, up, up_sib,
    lora, lora_far, down_own, up_own, sib, sib_end,
):
    rank, width, toks = up.shape[0], act.shape[1], act.shape[0]
    whole_low = rows2(whole_back(give, give_got), whole_back(give2, give_got2))
    out = (adapter_scale * nn(whole_low, rows2(up[...], up_sib[...]))).astype(bf16)
    lora[...] = out[:toks]
    lora_far[...] = out[toks:]
    grad = tn(whole_back(mine, got), rows2(act[...], act_got[...]))
    down_own[...] = grad[:rank]
    cut = sib.shape[1]
    sib[...] = grad[rank:, :cut].astype(bf16)
    sib_end[:, : width - cut] = grad[rank:, cut:].astype(bf16)
    grad = adapter_scale * tn(whole_low, rows2(cot[...], cot_got[: cot.shape[0], :]))
    up_own[...] = grad[:rank]
    sib_end[:, width - cut :] = grad[rank:].astype(bf16)


def adapter_end_kernel(where, down_own, up_own, got, got_end, down_out, up_out):
    cut, rest = got.shape[1], down_own.shape[1] - got.shape[1]
    down_out[0, :, :cut] = down_own[:, :cut] + got[...].astype(f32)
    down_out[0, :, cut:] = down_own[:, cut:] + got_end[:, :rest].astype(f32)
    up_out[0] = up_own[...] + got_end[:, rest:].astype(f32)


def base_near_kernel(where, act, act_got, weight, first, second, out):
    rows = weight.shape[0]
    head = rows - second.shape[0]
    cut = first.shape[0] - head
    wide = first.shape[1]
    at = pl.ds(pl.multiple_of(where[Y] * wide, wide), wide)
    near = rows2(act[:, at], act_got[:, at])
    out[:, :rows] = nt(rows2(act[...], act_got[...]), weight[...])
    out[:, rows : rows + head] = nt(near, first[cut:, :])
    out[:, rows + head :] = nt(near, second[...])


def base_far_kernel(where, part, act, act_got, first, second, low, low_got, keep, give, give2):
    rows = keep.shape[1]
    head = rows - second.shape[0]
    cut = first.shape[0] - head
    wide = first.shape[1]
    at = pl.ds(pl.multiple_of((1 - where[Y]) * wide, wide), wide)
    far = rows2(act[:, at], act_got[:, at])
    on_own = jnp.full((1, 1), where[ON_OWN], jnp.int32) == 1
    for lo, hi, block in ((0, head, first[cut:, :]), (head, rows, second[...])):
        mine = part[:, lo:hi]
        other = part[:, rows + lo : rows + hi] + nt(far, block)
        keep[:, lo:hi] = jnp.where(on_own, mine, other)
        out = jnp.where(on_own, other, mine).astype(bf16)
        give[:, lo:hi] = out[: give.shape[0]]
        give2[:, lo:hi] = out[give.shape[0] :]
    total = (low[...].astype(f32) + low_got[...].astype(f32)).astype(bf16)
    give[:, rows:] = total[: give.shape[0]]
    give2[:, rows:] = total[give.shape[0] :]


def held_kernel(where, keep, got, got2, here, there):
    toks = here.shape[0]
    held = (keep[...] + rows2(got[...], got2[...])[:, : keep.shape[1]].astype(f32)).astype(bf16)
    here[...] = held[:toks]
    there[...] = held[toks:]


def turn_kernel(where, held, got, lora_far, turn):
    in_pair = jnp.full((1, 1), where[IN_PAIR], jnp.int32) == 1
    base = held[...].astype(f32) + got[...].astype(f32)
    turn[...] = (lora_far[...].astype(f32) + jnp.where(in_pair, base, 0.0)).astype(bf16)


def output_kernel(where, held, got, lora, turned, out):
    in_pair = jnp.full((1, 1), where[IN_PAIR], jnp.int32) == 1
    base = held[...].astype(f32) + got[...].astype(f32)
    total = turned[...].astype(f32) + jnp.where(in_pair, base, 0.0)
    out[...] = (total + lora[...].astype(f32)).astype(bf16)


def pair_plan(
    activations,
    key_value_weight,
    token_adapter_index,
    adapter_down_weight,
    adapter_up_weight,
    cotangent,
):
    z = lax.axis_index("fsdp")
    y = lax.axis_index("groups")
    t = lax.axis_index("tp")
    x, c = t // 2, t % 2
    where = jnp.stack([y, z, x == z // 2, c == z % 2]).astype(jnp.int32)
    rows, width = key_value_weight.shape
    toks, out_width = cotangent.shape
    half, wide = rows // 2, width // 2
    down = adapter_down_weight[0]
    up = adapter_up_weight[0]
    rank = down.shape[0]
    places = [(zz, xx, cc) for zz in range(4) for xx in range(2) for cc in range(2)]

    idx = token_adapter_index.reshape(1, toks)
    idx_row = jnp.pad(idx.astype(bf16), ((0, 15), (0, out_width - toks)))
    cot_got = swap(jnp.concatenate([cotangent, idx_row], axis=0), "fsdp", 2)
    up_sib = swap(up, "fsdp", 1)
    head = rows * 2 // 4
    piece0 = column_half(where, wide, (down, key_value_weight), (rank, head), (0, 0))
    piece1 = column_half(where, wide, (key_value_weight,), (rows - head,), (1,))
    near0 = swap(piece0, "fsdp", 1)
    act_got = swap(after(activations, cot_got, up_sib), "fsdp", 2)
    near1 = swap(after(piece1, cot_got, up_sib), "fsdp", 1)

    mine, members = local_kernel(
        back_kernel,
        [((2 * toks, out_width + 2 * rank), bf16), ((2 * toks, 2 * rank), bf16)],
        where,
        cotangent, cot_got, idx, up, up_sib,
    )
    mine_x = swap(mine, "tp", 2)
    near0 = after(near0, mine)
    far0 = swap(near0, "groups", 1)
    far1 = swap(near1, "groups", 1)
    mine_x = after(mine_x, near1)
    mine = local_kernel(block_kernel, (mine.shape, bf16), where, mine, mine_x)
    got = swap(mine, "tp", 1)

    near, near_sent = gradient_half(where, y, mine, got, key_value_weight, down, near0, near1)
    near_got = swap(near_sent, "fsdp", 2)

    act_got = after(act_got, near_sent)
    part = local_kernel(
        base_near_kernel, ((2 * toks, 2 * rows), f32), where,
        activations, act_got, key_value_weight, near0, near1,
    )

    far0 = after(far0, part)
    low = low_part(where, activations, act_got, members, down, near0, far0)
    low_x = swap(low, "tp", 2)

    far1 = after(far1, low)
    far, far_sent = gradient_half(where, 1 - y, mine, got, key_value_weight, down, far0, far1)
    far_got = swap(far_sent, "fsdp", 2)

    part = after(part, far_sent)
    keep, give, give2 = local_kernel(
        base_far_kernel,
        [((2 * toks, rows), f32)] + [((toks, rows + 2 * rank), bf16)] * 2,
        where,
        part, activations, act_got, far0, far1, low, low_x,
    )
    keep, near_got = after((keep, near_got), give)
    give_got, give_got2 = swap(give, "tp", 1), swap(give2, "tp", 1)
    here, there = local_kernel(held_kernel, [((toks, rows), bf16)] * 2, where, keep, give_got, give_got2)
    inward = [((a, b, d), (a, 1 - b, d)) for a, b, d in places if b != a // 2]
    there_got = both(there, inward)
    here_got = both(here, inward)
    held = here

    give_got = after(give_got, held)
    lora, lora_far, down_own, up_own, sib, sib_end = local_kernel(
        adapter_kernel,
        [
            ((toks, out_width), bf16),
            ((toks, out_width), bf16),
            ((rank, width), f32),
            ((rank, out_width), f32),
            ((rank, (width + out_width) // 2), bf16),
            ((rank, (width + out_width) // 2), bf16),
        ],
        where,
        give, give2, give_got, give_got2, mine, got, activations, act_got, cotangent, cot_got, up, up_sib,
    )
    turn = local_kernel(
        turn_kernel, ((toks, out_width), bf16), where, there, there_got, lora_far
    )
    turned = swap(turn, "fsdp", 2)
    sib_got, sib_end_got = swap(sib, "fsdp", 1), swap(sib_end, "fsdp", 1)
    input_gradient = local_kernel(
        gradient_end_kernel, ((toks, width), bf16), where, near, near_got, far, far_got
    )
    key_value_output = local_kernel(
        output_kernel, ((toks, out_width), bf16), where, here, here_got, lora, turned
    )
    sib_got, sib_end_got = after((sib_got, sib_end_got), key_value_output)
    grad_down, up_gradient = local_kernel(
        adapter_end_kernel, [((1, rank, width), f32), ((1, rank, out_width), f32)], where,
        down_own, up_own, sib_got, sib_end_got,
    )

    return (key_value_output, input_gradient, grad_down, up_gradient)


def solution(mesh):
    paired = mesh.shape["fsdp"] == 4 and mesh.shape["tp"] == 4 and mesh.shape["groups"] == 2
    return jax.shard_map(
        pair_plan if paired else gathered_plan,
        mesh=mesh,
        in_specs=(
            P(("groups", "fsdp"), "tp"),
            P("fsdp", "tp"),
            P(("groups", "fsdp"), None),
            P("fsdp", None, "tp"),
            P("fsdp", None, "tp"),
            P(("groups", "fsdp"), "tp"),
        ),
        out_specs=(
            P(("groups", "fsdp"), "tp"),
            P(("groups", "fsdp"), "tp"),
            P(("groups", "fsdp"), None, "tp"),
            P(("groups", "fsdp"), None, "tp"),
        ),
        check_vma=False,
    )
```

```python
import jax
import jax.numpy as jnp
from jax import lax
from jax.experimental import pallas as pl
from jax.experimental.pallas import tpu as pltpu
from jax.sharding import PartitionSpec as P

adapter_scale = 2.0
f32 = jnp.float32
bf16 = jnp.bfloat16


def placement_matrix(token_adapter_index, adapter_holders, slot_capacity):
    owner_of = token_adapter_index[:, 0]
    shard_member = (
        owner_of[:, None] == jnp.arange(adapter_holders, dtype=jnp.int32)[None, :]
    ).astype(jnp.int32)
    earlier = jnp.cumsum(shard_member, axis=0) - shard_member
    within = jnp.sum(earlier * shard_member, axis=1)
    target = owner_of * slot_capacity + within
    return (
        jnp.arange(adapter_holders * slot_capacity, dtype=jnp.int32)[:, None] == target[None, :]
    ).astype(jnp.bfloat16)


def pack_rows(placing, values, adapter_holders):
    packed = jnp.dot(placing, values, preferred_element_type=jnp.float32).astype(jnp.bfloat16)
    return packed.reshape(adapter_holders, -1, values.shape[1])


def unpack_rows(placing, returned):
    flat = returned.reshape(-1, returned.shape[2])
    return jnp.einsum("st,sk->tk", placing, flat, preferred_element_type=jnp.float32)


def gathered_plan(
    activations,
    key_value_weight,
    token_adapter_index,
    adapter_down_weight,
    adapter_up_weight,
    cotangent,
):
    adapter_holders = lax.axis_size("fsdp")
    tok_rows = activations.shape[0]
    slot_capacity = 2 * tok_rows // adapter_holders
    feature_width = activations.shape[1]
    output_width = cotangent.shape[1]
    placing = placement_matrix(token_adapter_index, adapter_holders, slot_capacity)
    down_resident = adapter_down_weight[0]
    up_resident = adapter_up_weight[0]
    whole_cot = lax.all_gather(cotangent, "tp", axis=1, tiled=True)
    whole_weight = lax.all_gather(key_value_weight, "fsdp", axis=0, tiled=True)
    partial_value = jnp.dot(activations, whole_weight.T, preferred_element_type=jnp.float32)
    base_gradient = jnp.dot(whole_cot, whole_weight, preferred_element_type=jnp.float32)
    base_output = lax.psum_scatter(
        partial_value.astype(jnp.bfloat16), "tp", scatter_dimension=1, tiled=True
    ).astype(jnp.float32)
    rows_send = pack_rows(placing, activations, adapter_holders)
    cot_send = pack_rows(placing, cotangent, adapter_holders)
    rows_recv = lax.all_to_all(rows_send, "fsdp", split_axis=0, concat_axis=0, tiled=True)
    rows_flat = rows_recv.reshape(-1, feature_width)
    low_part = jnp.dot(rows_flat, down_resident.T, preferred_element_type=jnp.float32)
    rank_activation = lax.psum(low_part.astype(jnp.bfloat16), "tp")
    adapter_output = (
        adapter_scale * jnp.dot(rank_activation, up_resident, preferred_element_type=jnp.float32)
    ).astype(jnp.bfloat16)
    out_back = lax.all_to_all(
        adapter_output.reshape(adapter_holders, slot_capacity, output_width),
        "fsdp",
        split_axis=0,
        concat_axis=0,
        tiled=True,
    )
    cot_recv = lax.all_to_all(cot_send, "fsdp", split_axis=0, concat_axis=0, tiled=True)
    flat_output_gradient = cot_recv.reshape(-1, output_width)
    backward_piece = adapter_scale * jnp.dot(
        flat_output_gradient, up_resident.T, preferred_element_type=jnp.float32
    )
    backward_result = lax.psum(backward_piece.astype(jnp.bfloat16), "tp")
    adapter_input = jnp.dot(
        backward_result, down_resident, preferred_element_type=jnp.float32
    ).astype(jnp.bfloat16)
    in_back = lax.all_to_all(
        adapter_input.reshape(adapter_holders, slot_capacity, feature_width),
        "fsdp",
        split_axis=0,
        concat_axis=0,
        tiled=True,
    )
    grad_down = jnp.einsum(
        "sr,sd->rd", backward_result, rows_flat, preferred_element_type=jnp.float32
    )
    up_gradient = adapter_scale * jnp.einsum(
        "sr,sk->rk", rank_activation, flat_output_gradient, preferred_element_type=jnp.float32
    )
    key_value_output = (base_output + unpack_rows(placing, out_back)).astype(jnp.bfloat16)
    input_gradient = (base_gradient + unpack_rows(placing, in_back)).astype(jnp.bfloat16)
    return (key_value_output, input_gradient, grad_down[None], up_gradient[None])


def nn(a, b):
    return lax.dot_general(a, b, (((1,), (0,)), ((), ())), preferred_element_type=f32)


def nt(a, b):
    return lax.dot_general(a, b, (((1,), (1,)), ((), ())), preferred_element_type=f32)


def tn(a, b):
    return lax.dot_general(a, b, (((0,), (0,)), ((), ())), preferred_element_type=f32)


def rows2(a, b):
    return jnp.concatenate([a, b], axis=0)


def swap(x, axis, bit):
    return lax.ppermute(x, axis, [(i, i ^ bit) for i in range(lax.axis_size(axis))])


def both(x, pairs):
    flat = [(4 * a[0] + 2 * a[1] + a[2], 4 * b[0] + 2 * b[1] + b[2]) for a, b in pairs]
    return lax.ppermute(x, ("fsdp", "tp"), flat)


def after(values, *earlier):
    return lax.optimization_barrier((values, earlier))[0]


Y, Z, IN_PAIR, ON_OWN, OTHER_Y = range(5)


SMALL = pl.CostEstimate(flops=0, bytes_accessed=1000, transcendentals=0)


def local_kernel(body, outs, where, *args):
    single = not isinstance(outs, list)
    shapes = [jax.ShapeDtypeStruct(s, d) for s, d in ([outs] if single else outs)]
    got = pl.pallas_call(
        body,
        out_shape=shapes,
        in_specs=[pl.BlockSpec(memory_space=pltpu.SMEM)]
        + [pl.BlockSpec(memory_space=pltpu.VMEM)] * len(args),
        out_specs=[pl.BlockSpec(memory_space=pltpu.VMEM)] * len(shapes),
        compiler_params=pltpu.CompilerParams(vmem_limit_bytes=12 * 1024 * 1024),
        cost_estimate=SMALL,
    )(where, *args)
    return got[0] if single else got


def column_half(where, wide, arrays, counts, blocks):
    def body(where, *refs):
        place = 0
        for ref in refs[:-1]:
            refs[-1][place : place + ref.shape[0], :] = ref[...]
            place += ref.shape[0]

    def spec(count, block):
        return pl.BlockSpec((count, wide), lambda j, s: (block, s[Y]))

    total = sum(counts)
    return pl.pallas_call(
        body,
        grid_spec=pltpu.PrefetchScalarGridSpec(
            num_scalar_prefetch=1,
            grid=(1,),
            in_specs=[spec(n, b) for n, b in zip(counts, blocks)],
            out_specs=pl.BlockSpec((total, wide), lambda j, s: (0, 0)),
        ),
        out_shape=jax.ShapeDtypeStruct((total, wide), bf16),
        compiler_params=pltpu.CompilerParams(vmem_limit_bytes=12 * 1024 * 1024),
        cost_estimate=SMALL,
    )(where, *arrays)


def member(where, idx, rank):
    lane = lax.broadcasted_iota(jnp.int32, (idx.shape[0], 2 * rank), 1)
    z = where[Z]
    return idx == jnp.where(lane < rank, z, z ^ 1)


def column(row):
    n = row.shape[1]
    same = lax.broadcasted_iota(jnp.int32, (n, n), 0) == lax.broadcasted_iota(jnp.int32, (n, n), 1)
    picked = jnp.where(same, jnp.broadcast_to(row, (n, n)).astype(f32), 0.0)
    return jnp.sum(picked, axis=1, keepdims=True).astype(jnp.int32)


def back_kernel(where, cot, cot_got, idx, up, up_sib, out, members):
    width = cot.shape[1]
    toks = cot.shape[0]
    cot2 = rows2(cot[...], cot_got[:toks, :])
    part = adapter_scale * nt(cot2, rows2(up[...], up_sib[...]))
    idx_got = cot_got[toks:, :toks].astype(f32)[:1].astype(jnp.int32)
    mine = member(where, rows2(column(idx[...]), column(idx_got)), up.shape[0])
    members[...] = mine.astype(bf16)
    out[:, :width] = cot2
    out[:, width:] = jnp.where(mine, part, 0.0).astype(bf16)


def block_kernel(where, mine, got, out):
    width = out.shape[1] - 128
    in_pair = jnp.full((1, 1), where[IN_PAIR], jnp.int32) == 1
    out[:, :width] = jnp.where(in_pair, mine[:, :width], got[:, :width])
    out[:, width:] = (mine[:, width:].astype(f32) + got[:, width:].astype(f32)).astype(bf16)


def pair_blocks(where, mine, got):
    width = mine.shape[1] - 128
    on_own = jnp.full((1, 1), where[ON_OWN], jnp.int32) == 1
    a, b = mine[:, :width], got[:, :width]
    return jnp.where(on_own, a, b), jnp.where(on_own, b, a)


def whole_back(mine, got):
    width = mine.shape[1] - 128
    return (mine[:, width:].astype(f32) + got[:, width:].astype(f32)).astype(bf16)


def gradient_kernel(where, mine, got, weight, down, first, second, top, bottom):
    rank = down.shape[0]
    head = first.shape[0] - rank
    c_own, c_sib = pair_blocks(where, mine, got)
    back = whole_back(mine, got)
    g = nn(c_own, weight[...])
    g += nn(c_sib[:, :head], first[rank:, :])
    g += nn(c_sib[:, head:], second[...])
    g += nn(back, rows2(down[...], first[:rank, :]))
    toks = top.shape[0]
    top[...] = g[:toks].astype(bf16)
    bottom[...] = g[toks:].astype(bf16)


def gradient_half(where, side, mine, got, weight, down, first, second):
    toks, tile = mine.shape[0] // 2, 512
    steps = first.shape[1] // tile
    whole = lambda a: pl.BlockSpec(a.shape, lambda j, s: (0, 0))
    by_side = lambda a: pl.BlockSpec((a.shape[0], tile), lambda j, s: (0, s[side] * steps + j))
    tiled = lambda n: pl.BlockSpec((n, tile), lambda j, s: (0, j))
    return pl.pallas_call(
        gradient_kernel,
        grid_spec=pltpu.PrefetchScalarGridSpec(
            num_scalar_prefetch=1,
            grid=(steps,),
            in_specs=[
                whole(mine),
                whole(got),
                by_side(weight),
                by_side(down),
                tiled(first.shape[0]),
                tiled(second.shape[0]),
            ],
            out_specs=[tiled(toks), tiled(toks)],
        ),
        out_shape=[
            jax.ShapeDtypeStruct((toks, steps * tile), bf16),
            jax.ShapeDtypeStruct((toks, steps * tile), bf16),
        ],
        compiler_params=pltpu.CompilerParams(vmem_limit_bytes=20 * 1024 * 1024),
        cost_estimate=SMALL,
    )(where, mine, got, weight, down, first, second)


def gradient_end_kernel(where, near, near_got, far, far_got, out):
    half = near.shape[1]
    y = where[Y]
    at = pl.ds(pl.multiple_of(y * half, half), half)
    out[:, at] = (near[...].astype(f32) + near_got[...].astype(f32)).astype(bf16)
    at = pl.ds(pl.multiple_of((1 - y) * half, half), half)
    out[:, at] = (far[...].astype(f32) + far_got[...].astype(f32)).astype(bf16)


def low_kernel(where, act, act_got, members, down, near, far, out):
    rank, half = down.shape[0], near.shape[1]
    y = where[Y]
    at_near = pl.ds(pl.multiple_of(y * half, half), half)
    at_far = pl.ds(pl.multiple_of((1 - y) * half, half), half)
    part = nt(rows2(act[:, at_near], act_got[:, at_near]), rows2(down[:, at_near], near[:rank, :]))
    part += nt(rows2(act[:, at_far], act_got[:, at_far]), rows2(down[:, at_far], far[:rank, :]))
    out[...] = jnp.where(members[...] != 0, part, 0.0).astype(bf16)


def low_part(where, act, act_got, members, down, near, far):
    whole = lambda a: pl.BlockSpec(a.shape, lambda j: (0, 0))
    head = pl.BlockSpec((down.shape[0], near.shape[1]), lambda j: (0, 0))
    return pl.pallas_call(
        low_kernel,
        grid=(1,),
        in_specs=[pl.BlockSpec(memory_space=pltpu.SMEM)]
        + [whole(a) for a in (act, act_got, members, down)]
        + [head, head],
        out_specs=whole(members),
        out_shape=jax.ShapeDtypeStruct(members.shape, bf16),
        compiler_params=pltpu.CompilerParams(vmem_limit_bytes=12 * 1024 * 1024),
        cost_estimate=SMALL,
    )(where, act, act_got, members, down, near, far)


def adapter_kernel(
    where, give, give2, give_got, give_got2, mine, got, act, act_got, cot, cot_got, up, up_sib,
    lora, lora_far, down_own, up_own, sib, sib_end,
):
    rank, width, toks = up.shape[0], act.shape[1], act.shape[0]
    whole_low = rows2(whole_back(give, give_got), whole_back(give2, give_got2))
    out = (adapter_scale * nn(whole_low, rows2(up[...], up_sib[...]))).astype(bf16)
    lora[...] = out[:toks]
    lora_far[...] = out[toks:]
    grad = tn(whole_back(mine, got), rows2(act[...], act_got[...]))
    down_own[...] = grad[:rank]
    cut = sib.shape[1]
    sib[...] = grad[rank:, :cut].astype(bf16)
    sib_end[:, : width - cut] = grad[rank:, cut:].astype(bf16)
    grad = adapter_scale * tn(whole_low, rows2(cot[...], cot_got[: cot.shape[0], :]))
    up_own[...] = grad[:rank]
    sib_end[:, width - cut :] = grad[rank:].astype(bf16)


def adapter_end_kernel(where, down_own, up_own, got, got_end, down_out, up_out):
    cut, rest = got.shape[1], down_own.shape[1] - got.shape[1]
    down_out[0, :, :cut] = down_own[:, :cut] + got[...].astype(f32)
    down_out[0, :, cut:] = down_own[:, cut:] + got_end[:, :rest].astype(f32)
    up_out[0] = up_own[...] + got_end[:, rest:].astype(f32)


def base_near_kernel(where, act, act_got, weight, first, second, out):
    rows = weight.shape[0]
    head = rows - second.shape[0]
    cut = first.shape[0] - head
    wide = first.shape[1]
    at = pl.ds(pl.multiple_of(where[Y] * wide, wide), wide)
    near = rows2(act[:, at], act_got[:, at])
    out[:, :rows] = nt(rows2(act[...], act_got[...]), weight[...])
    out[:, rows : rows + head] = nt(near, first[cut:, :])
    out[:, rows + head :] = nt(near, second[...])


def base_far_kernel(where, part, act, act_got, first, second, low, low_got, keep, give, give2):
    rows = keep.shape[1]
    head = rows - second.shape[0]
    cut = first.shape[0] - head
    wide = first.shape[1]
    at = pl.ds(pl.multiple_of((1 - where[Y]) * wide, wide), wide)
    far = rows2(act[:, at], act_got[:, at])
    on_own = jnp.full((1, 1), where[ON_OWN], jnp.int32) == 1
    for lo, hi, block in ((0, head, first[cut:, :]), (head, rows, second[...])):
        mine = part[:, lo:hi]
        other = part[:, rows + lo : rows + hi] + nt(far, block)
        keep[:, lo:hi] = jnp.where(on_own, mine, other)
        out = jnp.where(on_own, other, mine).astype(bf16)
        give[:, lo:hi] = out[: give.shape[0]]
        give2[:, lo:hi] = out[give.shape[0] :]
    total = (low[...].astype(f32) + low_got[...].astype(f32)).astype(bf16)
    give[:, rows:] = total[: give.shape[0]]
    give2[:, rows:] = total[give.shape[0] :]


def held_kernel(where, keep, got, got2, here, there):
    toks = here.shape[0]
    held = (keep[...] + rows2(got[...], got2[...])[:, : keep.shape[1]].astype(f32)).astype(bf16)
    here[...] = held[:toks]
    there[...] = held[toks:]


def turn_kernel(where, held, got, lora_far, turn):
    in_pair = jnp.full((1, 1), where[IN_PAIR], jnp.int32) == 1
    base = held[...].astype(f32) + got[...].astype(f32)
    turn[...] = (lora_far[...].astype(f32) + jnp.where(in_pair, base, 0.0)).astype(bf16)


def output_kernel(where, held, got, lora, turned, out):
    in_pair = jnp.full((1, 1), where[IN_PAIR], jnp.int32) == 1
    base = held[...].astype(f32) + got[...].astype(f32)
    total = turned[...].astype(f32) + jnp.where(in_pair, base, 0.0)
    out[...] = (total + lora[...].astype(f32)).astype(bf16)


def pair_plan(
    activations,
    key_value_weight,
    token_adapter_index,
    adapter_down_weight,
    adapter_up_weight,
    cotangent,
):
    z = lax.axis_index("fsdp")
    y = lax.axis_index("groups")
    t = lax.axis_index("tp")
    x, c = t // 2, t % 2
    where = jnp.stack([y, z, x == z // 2, c == z % 2, 1 - y]).astype(jnp.int32)
    rows, width = key_value_weight.shape
    toks, out_width = cotangent.shape
    half, wide = rows // 2, width // 2
    down = adapter_down_weight[0]
    up = adapter_up_weight[0]
    rank = down.shape[0]
    places = [(zz, xx, cc) for zz in range(4) for xx in range(2) for cc in range(2)]

    idx = token_adapter_index.reshape(1, toks)
    idx_row = jnp.pad(idx.astype(bf16), ((0, 15), (0, out_width - toks)))
    cot_got = swap(jnp.concatenate([cotangent, idx_row], axis=0), "fsdp", 2)
    up_sib = swap(up, "fsdp", 1)
    head = rows * 2 // 4
    piece0 = column_half(where, wide, (down, key_value_weight), (rank, head), (0, 0))
    piece1 = column_half(where, wide, (key_value_weight,), (rows - head,), (1,))
    near0 = swap(piece0, "fsdp", 1)
    act_got = swap(after(activations, cot_got, up_sib), "fsdp", 2)
    near1 = swap(after(piece1, cot_got, up_sib), "fsdp", 1)

    mine, members = local_kernel(
        back_kernel,
        [((2 * toks, out_width + 2 * rank), bf16), ((2 * toks, 2 * rank), bf16)],
        where,
        cotangent, cot_got, idx, up, up_sib,
    )
    mine_x = swap(mine, "tp", 2)
    near0 = after(near0, mine)
    far0 = swap(near0, "groups", 1)
    far1 = swap(near1, "groups", 1)
    mine_x = after(mine_x, near1)
    mine = local_kernel(block_kernel, (mine.shape, bf16), where, mine, mine_x)
    got = swap(mine, "tp", 1)

    near, near_sent = gradient_half(where, Y, mine, got, key_value_weight, down, near0, near1)
    near_got = swap(near_sent, "fsdp", 2)

    act_got = after(act_got, near_sent)
    part = local_kernel(
        base_near_kernel, ((2 * toks, 2 * rows), f32), where,
        activations, act_got, key_value_weight, near0, near1,
    )

    far0 = after(far0, part)
    low = low_part(where, activations, act_got, members, down, near0, far0)
    low_x = swap(low, "tp", 2)

    far1 = after(far1, low)
    far, far_sent = gradient_half(where, OTHER_Y, mine, got, key_value_weight, down, far0, far1)
    far_got = swap(far_sent, "fsdp", 2)

    part = after(part, far_sent)
    keep, give, give2 = local_kernel(
        base_far_kernel,
        [((2 * toks, rows), f32)] + [((toks, rows + 2 * rank), bf16)] * 2,
        where,
        part, activations, act_got, far0, far1, low, low_x,
    )
    keep, near_got = after((keep, near_got), give)
    give_got, give_got2 = swap(give, "tp", 1), swap(give2, "tp", 1)
    here, there = local_kernel(held_kernel, [((toks, rows), bf16)] * 2, where, keep, give_got, give_got2)
    inward = [((a, b, d), (a, 1 - b, d)) for a, b, d in places if b != a // 2]
    there_got = both(there, inward)
    here_got = both(here, inward)
    held = here

    give_got = after(give_got, held)
    lora, lora_far, down_own, up_own, sib, sib_end = local_kernel(
        adapter_kernel,
        [
            ((toks, out_width), bf16),
            ((toks, out_width), bf16),
            ((rank, width), f32),
            ((rank, out_width), f32),
            ((rank, (width + out_width) // 2), bf16),
            ((rank, (width + out_width) // 2), bf16),
        ],
        where,
        give, give2, give_got, give_got2, mine, got, activations, act_got, cotangent, cot_got, up, up_sib,
    )
    turn = local_kernel(
        turn_kernel, ((toks, out_width), bf16), where, there, there_got, lora_far
    )
    turned = swap(turn, "fsdp", 2)
    sib_got, sib_end_got = swap(sib, "fsdp", 1), swap(sib_end, "fsdp", 1)
    input_gradient = local_kernel(
        gradient_end_kernel, ((toks, width), bf16), where, near, near_got, far, far_got
    )
    key_value_output = local_kernel(
        output_kernel, ((toks, out_width), bf16), where, here, here_got, lora, turned
    )
    sib_got, sib_end_got = after((sib_got, sib_end_got), key_value_output)
    grad_down, up_gradient = local_kernel(
        adapter_end_kernel, [((1, rank, width), f32), ((1, rank, out_width), f32)], where,
        down_own, up_own, sib_got, sib_end_got,
    )

    return (key_value_output, input_gradient, grad_down, up_gradient)


def solution(mesh):
    paired = mesh.shape["fsdp"] == 4 and mesh.shape["tp"] == 4 and mesh.shape["groups"] == 2
    return jax.shard_map(
        pair_plan if paired else gathered_plan,
        mesh=mesh,
        in_specs=(
            P(("groups", "fsdp"), "tp"),
            P("fsdp", "tp"),
            P(("groups", "fsdp"), None),
            P("fsdp", None, "tp"),
            P("fsdp", None, "tp"),
            P(("groups", "fsdp"), "tp"),
        ),
        out_specs=(
            P(("groups", "fsdp"), "tp"),
            P(("groups", "fsdp"), "tp"),
            P(("groups", "fsdp"), None, "tp"),
            P(("groups", "fsdp"), None, "tp"),
        ),
        check_vma=False,
    )
```

```python
import jax
import jax.numpy as jnp
from jax import lax
from jax.experimental import pallas as pl
from jax.experimental.pallas import tpu as pltpu
from jax.sharding import PartitionSpec as P

adapter_scale = 2.0
f32 = jnp.float32
bf16 = jnp.bfloat16


def placement_matrix(token_adapter_index, adapter_holders, slot_capacity):
    owner_of = token_adapter_index[:, 0]
    shard_member = (
        owner_of[:, None] == jnp.arange(adapter_holders, dtype=jnp.int32)[None, :]
    ).astype(jnp.int32)
    earlier = jnp.cumsum(shard_member, axis=0) - shard_member
    within = jnp.sum(earlier * shard_member, axis=1)
    target = owner_of * slot_capacity + within
    return (
        jnp.arange(adapter_holders * slot_capacity, dtype=jnp.int32)[:, None] == target[None, :]
    ).astype(jnp.bfloat16)


def pack_rows(placing, values, adapter_holders):
    packed = jnp.dot(placing, values, preferred_element_type=jnp.float32).astype(jnp.bfloat16)
    return packed.reshape(adapter_holders, -1, values.shape[1])


def unpack_rows(placing, returned):
    flat = returned.reshape(-1, returned.shape[2])
    return jnp.einsum("st,sk->tk", placing, flat, preferred_element_type=jnp.float32)


def gathered_plan(
    activations,
    key_value_weight,
    token_adapter_index,
    adapter_down_weight,
    adapter_up_weight,
    cotangent,
):
    adapter_holders = lax.axis_size("fsdp")
    tok_rows = activations.shape[0]
    slot_capacity = 2 * tok_rows // adapter_holders
    feature_width = activations.shape[1]
    output_width = cotangent.shape[1]
    placing = placement_matrix(token_adapter_index, adapter_holders, slot_capacity)
    down_resident = adapter_down_weight[0]
    up_resident = adapter_up_weight[0]
    whole_cot = lax.all_gather(cotangent, "tp", axis=1, tiled=True)
    whole_weight = lax.all_gather(key_value_weight, "fsdp", axis=0, tiled=True)
    partial_value = jnp.dot(activations, whole_weight.T, preferred_element_type=jnp.float32)
    base_gradient = jnp.dot(whole_cot, whole_weight, preferred_element_type=jnp.float32)
    base_output = lax.psum_scatter(
        partial_value.astype(jnp.bfloat16), "tp", scatter_dimension=1, tiled=True
    ).astype(jnp.float32)
    rows_send = pack_rows(placing, activations, adapter_holders)
    cot_send = pack_rows(placing, cotangent, adapter_holders)
    rows_recv = lax.all_to_all(rows_send, "fsdp", split_axis=0, concat_axis=0, tiled=True)
    rows_flat = rows_recv.reshape(-1, feature_width)
    low_part = jnp.dot(rows_flat, down_resident.T, preferred_element_type=jnp.float32)
    rank_activation = lax.psum(low_part.astype(jnp.bfloat16), "tp")
    adapter_output = (
        adapter_scale * jnp.dot(rank_activation, up_resident, preferred_element_type=jnp.float32)
    ).astype(jnp.bfloat16)
    out_back = lax.all_to_all(
        adapter_output.reshape(adapter_holders, slot_capacity, output_width),
        "fsdp",
        split_axis=0,
        concat_axis=0,
        tiled=True,
    )
    cot_recv = lax.all_to_all(cot_send, "fsdp", split_axis=0, concat_axis=0, tiled=True)
    flat_output_gradient = cot_recv.reshape(-1, output_width)
    backward_piece = adapter_scale * jnp.dot(
        flat_output_gradient, up_resident.T, preferred_element_type=jnp.float32
    )
    backward_result = lax.psum(backward_piece.astype(jnp.bfloat16), "tp")
    adapter_input = jnp.dot(
        backward_result, down_resident, preferred_element_type=jnp.float32
    ).astype(jnp.bfloat16)
    in_back = lax.all_to_all(
        adapter_input.reshape(adapter_holders, slot_capacity, feature_width),
        "fsdp",
        split_axis=0,
        concat_axis=0,
        tiled=True,
    )
    grad_down = jnp.einsum(
        "sr,sd->rd", backward_result, rows_flat, preferred_element_type=jnp.float32
    )
    up_gradient = adapter_scale * jnp.einsum(
        "sr,sk->rk", rank_activation, flat_output_gradient, preferred_element_type=jnp.float32
    )
    key_value_output = (base_output + unpack_rows(placing, out_back)).astype(jnp.bfloat16)
    input_gradient = (base_gradient + unpack_rows(placing, in_back)).astype(jnp.bfloat16)
    return (key_value_output, input_gradient, grad_down[None], up_gradient[None])


def nn(a, b):
    return lax.dot_general(a, b, (((1,), (0,)), ((), ())), preferred_element_type=f32)


def nt(a, b):
    return lax.dot_general(a, b, (((1,), (1,)), ((), ())), preferred_element_type=f32)


def tn(a, b):
    return lax.dot_general(a, b, (((0,), (0,)), ((), ())), preferred_element_type=f32)


def rows2(a, b):
    return jnp.concatenate([a, b], axis=0)


def swap(x, axis, bit):
    return lax.ppermute(x, axis, [(i, i ^ bit) for i in range(lax.axis_size(axis))])


def both(x, pairs):
    flat = [(4 * a[0] + 2 * a[1] + a[2], 4 * b[0] + 2 * b[1] + b[2]) for a, b in pairs]
    return lax.ppermute(x, ("fsdp", "tp"), flat)


def after(values, *earlier):
    return lax.optimization_barrier((values, earlier))[0]


Y, Z, IN_PAIR, ON_OWN, OTHER_Y = range(5)


SMALL = pl.CostEstimate(flops=0, bytes_accessed=1000, transcendentals=0)


def local_kernel(body, outs, where, *args):
    single = not isinstance(outs, list)
    shapes = [jax.ShapeDtypeStruct(s, d) for s, d in ([outs] if single else outs)]
    got = pl.pallas_call(
        body,
        out_shape=shapes,
        in_specs=[pl.BlockSpec(memory_space=pltpu.SMEM)]
        + [pl.BlockSpec(memory_space=pltpu.VMEM)] * len(args),
        out_specs=[pl.BlockSpec(memory_space=pltpu.VMEM)] * len(shapes),
        compiler_params=pltpu.CompilerParams(vmem_limit_bytes=12 * 1024 * 1024),
        cost_estimate=SMALL,
    )(where, *args)
    return got[0] if single else got


def column_half(where, wide, arrays, counts, blocks):
    def body(where, *refs):
        place = 0
        for ref in refs[:-1]:
            refs[-1][place : place + ref.shape[0], :] = ref[...]
            place += ref.shape[0]

    def spec(count, block):
        return pl.BlockSpec((count, wide), lambda j, s: (block, s[Y]))

    total = sum(counts)
    return pl.pallas_call(
        body,
        grid_spec=pltpu.PrefetchScalarGridSpec(
            num_scalar_prefetch=1,
            grid=(1,),
            in_specs=[spec(n, b) for n, b in zip(counts, blocks)],
            out_specs=pl.BlockSpec((total, wide), lambda j, s: (0, 0)),
        ),
        out_shape=jax.ShapeDtypeStruct((total, wide), bf16),
        compiler_params=pltpu.CompilerParams(vmem_limit_bytes=12 * 1024 * 1024),
        cost_estimate=SMALL,
    )(where, *arrays)


def member(where, idx, rank):
    lane = lax.broadcasted_iota(jnp.int32, (idx.shape[0], 2 * rank), 1)
    z = where[Z]
    return idx == jnp.where(lane < rank, z, z ^ 1)


def column(row):
    n = row.shape[1]
    same = lax.broadcasted_iota(jnp.int32, (n, n), 0) == lax.broadcasted_iota(jnp.int32, (n, n), 1)
    picked = jnp.where(same, jnp.broadcast_to(row, (n, n)).astype(f32), 0.0)
    return jnp.sum(picked, axis=1, keepdims=True).astype(jnp.int32)


def back_kernel(where, cot, cot_got, idx, up, up_sib, out, members):
    width = cot.shape[1]
    toks = cot.shape[0]
    cot2 = rows2(cot[...], cot_got[:toks, :])
    part = adapter_scale * nt(cot2, rows2(up[...], up_sib[...]))
    idx_got = cot_got[toks:, :toks].astype(f32)[:1].astype(jnp.int32)
    mine = member(where, rows2(column(idx[...]), column(idx_got)), up.shape[0])
    members[...] = mine.astype(bf16)
    out[:, :width] = cot2
    out[:, width:] = jnp.where(mine, part, 0.0).astype(bf16)


def block_kernel(where, mine, got, out):
    width = out.shape[1] - 128
    in_pair = jnp.full((1, 1), where[IN_PAIR], jnp.int32) == 1
    out[:, :width] = jnp.where(in_pair, mine[:, :width], got[:, :width])
    out[:, width:] = (mine[:, width:].astype(f32) + got[:, width:].astype(f32)).astype(bf16)


def pair_blocks(where, mine, got):
    width = mine.shape[1] - 128
    on_own = jnp.full((1, 1), where[ON_OWN], jnp.int32) == 1
    a, b = mine[:, :width], got[:, :width]
    return jnp.where(on_own, a, b), jnp.where(on_own, b, a)


def whole_back(mine, got):
    width = mine.shape[1] - 128
    return (mine[:, width:].astype(f32) + got[:, width:].astype(f32)).astype(bf16)


def gradient_kernel(where, mine, got, weight, down, first, second, top, bottom):
    rank = down.shape[0]
    head = first.shape[0] - rank
    c_own, c_sib = pair_blocks(where, mine, got)
    back = whole_back(mine, got)
    g = nn(c_own, weight[...])
    g += nn(c_sib[:, :head], first[rank:, :])
    g += nn(c_sib[:, head:], second[...])
    g += nn(back, rows2(down[...], first[:rank, :]))
    toks = top.shape[0]
    top[...] = g[:toks].astype(bf16)
    bottom[...] = g[toks:].astype(bf16)


def gradient_half(where, side, mine, got, weight, down, first, second):
    toks, tile = mine.shape[0] // 2, 512
    steps = first.shape[1] // tile
    whole = lambda a: pl.BlockSpec(a.shape, lambda j, s: (0, 0))
    by_side = lambda a: pl.BlockSpec((a.shape[0], tile), lambda j, s: (0, s[side] * steps + j))
    tiled = lambda n: pl.BlockSpec((n, tile), lambda j, s: (0, j))
    return pl.pallas_call(
        gradient_kernel,
        grid_spec=pltpu.PrefetchScalarGridSpec(
            num_scalar_prefetch=1,
            grid=(steps,),
            in_specs=[
                whole(mine),
                whole(got),
                by_side(weight),
                by_side(down),
                tiled(first.shape[0]),
                tiled(second.shape[0]),
            ],
            out_specs=[tiled(toks), tiled(toks)],
        ),
        out_shape=[
            jax.ShapeDtypeStruct((toks, steps * tile), bf16),
            jax.ShapeDtypeStruct((toks, steps * tile), bf16),
        ],
        compiler_params=pltpu.CompilerParams(vmem_limit_bytes=20 * 1024 * 1024),
        cost_estimate=SMALL,
    )(where, mine, got, weight, down, first, second)


def gradient_end_kernel(where, near, near_got, far, far_got, out):
    half = near.shape[1]
    y = where[Y]
    at = pl.ds(pl.multiple_of(y * half, half), half)
    out[:, at] = (near[...].astype(f32) + near_got[...].astype(f32)).astype(bf16)
    at = pl.ds(pl.multiple_of((1 - y) * half, half), half)
    out[:, at] = (far[...].astype(f32) + far_got[...].astype(f32)).astype(bf16)


def low_kernel(where, act, act_got, members, down, near, far, out):
    rank, half = down.shape[0], near.shape[1]
    y = where[Y]
    at_near = pl.ds(pl.multiple_of(y * half, half), half)
    at_far = pl.ds(pl.multiple_of((1 - y) * half, half), half)
    part = nt(rows2(act[:, at_near], act_got[:, at_near]), rows2(down[:, at_near], near[:rank, :]))
    part += nt(rows2(act[:, at_far], act_got[:, at_far]), rows2(down[:, at_far], far[:rank, :]))
    out[...] = jnp.where(members[...] != 0, part, 0.0).astype(bf16)


def low_part(where, act, act_got, members, down, near, far):
    whole = lambda a: pl.BlockSpec(a.shape, lambda j: (0, 0))
    head = pl.BlockSpec((down.shape[0], near.shape[1]), lambda j: (0, 0))
    return pl.pallas_call(
        low_kernel,
        grid=(1,),
        in_specs=[pl.BlockSpec(memory_space=pltpu.SMEM)]
        + [whole(a) for a in (act, act_got, members, down)]
        + [head, head],
        out_specs=whole(members),
        out_shape=jax.ShapeDtypeStruct(members.shape, bf16),
        compiler_params=pltpu.CompilerParams(vmem_limit_bytes=12 * 1024 * 1024),
        cost_estimate=SMALL,
    )(where, act, act_got, members, down, near, far)


def adapter_kernel(
    where, give, give2, give_got, give_got2, mine, got, act, act_got, cot, cot_got, up, up_sib,
    lora, lora_far, down_own, up_own, sib, sib_end,
):
    rank, width, toks = up.shape[0], act.shape[1], act.shape[0]
    whole_low = rows2(whole_back(give, give_got), whole_back(give2, give_got2))
    out = (adapter_scale * nn(whole_low, rows2(up[...], up_sib[...]))).astype(bf16)
    lora[...] = out[:toks]
    lora_far[...] = out[toks:]
    grad = tn(whole_back(mine, got), rows2(act[...], act_got[...]))
    down_own[...] = grad[:rank]
    cut = sib.shape[1]
    sib[...] = grad[rank:, :cut].astype(bf16)
    sib_end[:, : width - cut] = grad[rank:, cut:].astype(bf16)
    grad = adapter_scale * tn(whole_low, rows2(cot[...], cot_got[: cot.shape[0], :]))
    up_own[...] = grad[:rank]
    sib_end[:, width - cut :] = grad[rank:].astype(bf16)


def adapter_end_kernel(where, down_own, up_own, got, got_end, down_out, up_out):
    cut, rest = got.shape[1], down_own.shape[1] - got.shape[1]
    down_out[0, :, :cut] = down_own[:, :cut] + got[...].astype(f32)
    down_out[0, :, cut:] = down_own[:, cut:] + got_end[:, :rest].astype(f32)
    up_out[0] = up_own[...] + got_end[:, rest:].astype(f32)


def base_near_kernel(where, act, act_got, weight, first, second, out):
    rows = weight.shape[0]
    head = rows - second.shape[0]
    cut = first.shape[0] - head
    wide = first.shape[1]
    at = pl.ds(pl.multiple_of(where[Y] * wide, wide), wide)
    near = rows2(act[:, at], act_got[:, at])
    out[:, :rows] = nt(rows2(act[...], act_got[...]), weight[...])
    out[:, rows : rows + head] = nt(near, first[cut:, :])
    out[:, rows + head :] = nt(near, second[...])


def base_far_kernel(where, part, act, act_got, first, second, low, low_got, keep, give, give2):
    rows = keep.shape[1]
    head = rows - second.shape[0]
    cut = first.shape[0] - head
    wide = first.shape[1]
    at = pl.ds(pl.multiple_of((1 - where[Y]) * wide, wide), wide)
    far = rows2(act[:, at], act_got[:, at])
    on_own = jnp.full((1, 1), where[ON_OWN], jnp.int32) == 1
    for lo, hi, block in ((0, head, first[cut:, :]), (head, rows, second[...])):
        mine = part[:, lo:hi]
        other = part[:, rows + lo : rows + hi] + nt(far, block)
        keep[:, lo:hi] = jnp.where(on_own, mine, other)
        out = jnp.where(on_own, other, mine).astype(bf16)
        give[:, lo:hi] = out[: give.shape[0]]
        give2[:, lo:hi] = out[give.shape[0] :]
    total = (low[...].astype(f32) + low_got[...].astype(f32)).astype(bf16)
    give[:, rows:] = total[: give.shape[0]]
    give2[:, rows:] = total[give.shape[0] :]


def held_kernel(where, keep, got, got2, here, there):
    toks = here.shape[0]
    held = (keep[...] + rows2(got[...], got2[...])[:, : keep.shape[1]].astype(f32)).astype(bf16)
    here[...] = held[:toks]
    there[...] = held[toks:]


def turn_kernel(where, held, got, lora_far, turn):
    in_pair = jnp.full((1, 1), where[IN_PAIR], jnp.int32) == 1
    base = held[...].astype(f32) + got[...].astype(f32)
    turn[...] = (lora_far[...].astype(f32) + jnp.where(in_pair, base, 0.0)).astype(bf16)


def output_kernel(where, held, got, lora, turned, out):
    in_pair = jnp.full((1, 1), where[IN_PAIR], jnp.int32) == 1
    base = held[...].astype(f32) + got[...].astype(f32)
    total = turned[...].astype(f32) + jnp.where(in_pair, base, 0.0)
    out[...] = (total + lora[...].astype(f32)).astype(bf16)


def pair_plan(
    activations,
    key_value_weight,
    token_adapter_index,
    adapter_down_weight,
    adapter_up_weight,
    cotangent,
):
    z = lax.axis_index("fsdp")
    y = lax.axis_index("groups")
    t = lax.axis_index("tp")
    x, c = t // 2, t % 2
    where = jnp.stack([y, z, x == z // 2, c == z % 2, 1 - y]).astype(jnp.int32)
    rows, width = key_value_weight.shape
    toks, out_width = cotangent.shape
    half, wide = rows // 2, width // 2
    down = adapter_down_weight[0]
    up = adapter_up_weight[0]
    rank = down.shape[0]
    places = [(zz, xx, cc) for zz in range(4) for xx in range(2) for cc in range(2)]

    idx = token_adapter_index.reshape(1, toks)
    idx_row = jnp.pad(idx.astype(bf16), ((0, 15), (0, out_width - toks)))
    cot_got = swap(jnp.concatenate([cotangent, idx_row], axis=0), "fsdp", 2)
    up_sib = swap(up, "fsdp", 1)
    head = rows * 2 // 4
    piece0 = column_half(where, wide, (down, key_value_weight), (rank, head), (0, 0))
    piece1 = column_half(where, wide, (key_value_weight,), (rows - head,), (1,))
    near0 = swap(piece0, "fsdp", 1)
    act_got = swap(after(activations, cot_got, up_sib), "fsdp", 2)
    near1 = swap(after(piece1, cot_got, up_sib), "fsdp", 1)

    mine, members = local_kernel(
        back_kernel,
        [((2 * toks, out_width + 2 * rank), bf16), ((2 * toks, 2 * rank), bf16)],
        where,
        cotangent, cot_got, idx, up, up_sib,
    )
    mine_x = swap(mine, "tp", 2)
    near0 = after(near0, mine)
    far0 = swap(near0, "groups", 1)
    far1 = swap(near1, "groups", 1)
    mine_x = after(mine_x, near1)
    mine = local_kernel(block_kernel, (mine.shape, bf16), where, mine, mine_x)
    got = swap(mine, "tp", 1)

    near, near_sent = gradient_half(where, Y, mine, got, key_value_weight, down, near0, near1)
    near_got = swap(near_sent, "fsdp", 2)

    act_got = after(act_got, near_sent)
    part = local_kernel(
        base_near_kernel, ((2 * toks, 2 * rows), f32), where,
        activations, act_got, key_value_weight, near0, near1,
    )

    far0 = after(far0, part)
    low = low_part(where, activations, act_got, members, down, near0, far0)
    low_x = swap(low, "tp", 2)

    far1 = after(far1, low)
    far, far_sent = gradient_half(where, OTHER_Y, mine, got, key_value_weight, down, far0, far1)
    far_got = swap(far_sent, "fsdp", 2)

    part = after(part, far_sent)
    keep, give, give2 = local_kernel(
        base_far_kernel,
        [((2 * toks, rows), f32)] + [((toks, rows + 2 * rank), bf16)] * 2,
        where,
        part, activations, act_got, far0, far1, low, low_x,
    )
    keep, near_got = after((keep, near_got), give)
    give_got, give_got2 = swap(give, "tp", 1), swap(give2, "tp", 1)
    here, there = local_kernel(held_kernel, [((toks, rows), bf16)] * 2, where, keep, give_got, give_got2)
    inward = [((a, b, d), (a, 1 - b, d)) for a, b, d in places if b != a // 2]
    there_got = both(there, inward)
    here_got = both(here, inward)
    held = here

    give_got = after(give_got, held)
    lora, lora_far, down_own, up_own, sib, sib_end = local_kernel(
        adapter_kernel,
        [
            ((toks, out_width), bf16),
            ((toks, out_width), bf16),
            ((rank, width), f32),
            ((rank, out_width), f32),
            ((rank, (width + out_width) // 2), bf16),
            ((rank, (width + out_width) // 2), bf16),
        ],
        where,
        give, give2, give_got, give_got2, mine, got, activations, act_got, cotangent, cot_got, up, up_sib,
    )
    turn = local_kernel(
        turn_kernel, ((toks, out_width), bf16), where, there, there_got, lora_far
    )
    turned = swap(turn, "fsdp", 2)
    sib_got, sib_end_got = swap(sib, "fsdp", 1), swap(sib_end, "fsdp", 1)
    input_gradient = local_kernel(
        gradient_end_kernel, ((toks, width), bf16), where, near, near_got, far, far_got
    )
    key_value_output = local_kernel(
        output_kernel, ((toks, out_width), bf16), where, here, here_got, lora, turned
    )
    sib_got, sib_end_got = after((sib_got, sib_end_got), input_gradient)
    grad_down, up_gradient = local_kernel(
        adapter_end_kernel, [((1, rank, width), f32), ((1, rank, out_width), f32)], where,
        down_own, up_own, sib_got, sib_end_got,
    )

    return (key_value_output, input_gradient, grad_down, up_gradient)


def solution(mesh):
    paired = mesh.shape["fsdp"] == 4 and mesh.shape["tp"] == 4 and mesh.shape["groups"] == 2
    return jax.shard_map(
        pair_plan if paired else gathered_plan,
        mesh=mesh,
        in_specs=(
            P(("groups", "fsdp"), "tp"),
            P("fsdp", "tp"),
            P(("groups", "fsdp"), None),
            P("fsdp", None, "tp"),
            P("fsdp", None, "tp"),
            P(("groups", "fsdp"), "tp"),
        ),
        out_specs=(
            P(("groups", "fsdp"), "tp"),
            P(("groups", "fsdp"), "tp"),
            P(("groups", "fsdp"), None, "tp"),
            P(("groups", "fsdp"), None, "tp"),
        ),
        check_vma=False,
    )
```
